32 devices in a mesh: seq: 8 (over y, x, core), head: 4 (over z).
Axes of the slice: x: 2, y: 2, z: 4, core: 2. Of those that a mesh axis runs over, the one named last changes fastest.
Arguments:
- queries: bfloat16 [3072, 3072], P('seq', 'head'), may hold values from -8 to 8
- key_states: bfloat16 [3072, 3072], P('seq', 'head'), may hold values from -8 to 8
- value_states: bfloat16 [3072, 3072], P('seq', 'head'), may hold values from -6 to 6
- block_lists: int32 [24, 4], replicated, may hold values from 0 to 23, as said below
- out_weight: bfloat16 [3072, 3072], P('head'), may hold values from -0.15625 to 0.15625
- out_grad: bfloat16 [3072, 3072], P('seq', 'head'), may hold values from -6 to 6
Outputs:
- attended: bfloat16 [3072, 3072], P('seq', 'head')
- query_grad: bfloat16 [3072, 3072], P('seq', 'head')
- key_grad: bfloat16 [3072, 3072], P('seq', 'head')
- value_grad: bfloat16 [3072, 3072], P('seq', 'head')
The draws below stay inside these ranges and needn't reach their ends.
Inputs may be any that keep to these rules, and one draw needn't show every extreme that they name: `block_lists`: row r names 4 different blocks, among them block r itself; 2 of them lie in r's own group of 3 blocks and 2 in other groups. Of each group's blocks at most two are named by rows of other groups, and the rows of one group name at most one block of any other group.
All inputs are finite; a program needn't handle non-finite values.
Results may differ from the reference program's by a relative error of at most 0.035.
Values may be sent and summed in bfloat16 or wider, within the bound.
A program may use at most 192 MiB of HBM per device.

```python
import math
import jax
import jax.numpy as jnp
from jax import lax

D = 3072
HEADS = 24
HD = 128
BLK = 128
LOCQ = 2
REMQ = 2
K_SEL = 4
QB_DEV = 3
GROUPS = 8
NQB = 24
CELLS = 3072
N_HEAD = 4


def base_rows(key, salt):
    noise_key = jax.random.fold_in(key, salt)
    return jnp.clip(1.6 * jax.random.normal(noise_key, (CELLS, HEADS * HD), jnp.float32), -8.0, 8.0)


def draw_queries(key, part):
    row_values = base_rows(key, 11)
    return row_values.astype(jnp.bfloat16)


def draw_key_states(key, part):
    row_values = base_rows(key, 12)
    return row_values.astype(jnp.bfloat16)


def draw_block_lists(key, part):
    port_key = jax.random.fold_in(key, 201)
    pick_key = jax.random.fold_in(key, 202)
    remote_key = jax.random.fold_in(key, 203)
    local_key = jax.random.fold_in(key, 204)
    special_key = jax.random.fold_in(key, 205)
    forced_key = jax.random.fold_in(key, 206)
    order_key = jax.random.fold_in(key, 207)
    first_port = jax.random.randint(port_key, (GROUPS,), 0, QB_DEV)
    second_port = (first_port + jax.random.randint(jax.random.fold_in(port_key, 1), (GROUPS,), 1, QB_DEV)) % QB_DEV
    port_pairs = jnp.stack([first_port, second_port], axis=1).astype(jnp.int32)
    group_ids = jnp.arange(GROUPS, dtype=jnp.int32)
    port_picks = jax.random.randint(pick_key, (GROUPS, GROUPS), 0, 2).astype(jnp.int32)
    port_picks = port_picks.at[group_ids, (group_ids + 1) % GROUPS].set(0)
    port_picks = port_picks.at[group_ids, (group_ids + 2) % GROUPS].set(1)
    row_ids = jnp.arange(NQB, dtype=jnp.int32)
    groups_of = row_ids // QB_DEV
    inner_index = row_ids % QB_DEV
    special = jax.random.randint(special_key, (GROUPS,), 0, QB_DEV).astype(jnp.int32)
    drawn_steps = jax.vmap(lambda sub_key: jax.random.permutation(sub_key, GROUPS - 1)[:REMQ] + 1)(jax.random.split(remote_key, NQB)).astype(jnp.int32)
    forced_tail = jax.vmap(lambda sub_key: jax.random.permutation(sub_key, GROUPS - 3)[:REMQ - 2] + 3)(jax.random.split(forced_key, NQB)).astype(jnp.int32)
    forced = jnp.concatenate([jnp.broadcast_to(jnp.array([1, 2], jnp.int32), (NQB, 2)), forced_tail], axis=1)
    is_special = (inner_index == special[groups_of])[:, None]
    offsets = jnp.where(is_special, forced, drawn_steps)
    owners = (groups_of[:, None] + offsets) % GROUPS
    chosen = port_picks[groups_of[:, None], owners]
    far_blocks = owners * QB_DEV + port_pairs[owners, chosen]
    near_steps = jax.vmap(lambda sub_key: jax.random.permutation(sub_key, QB_DEV - 1)[:LOCQ - 1] + 1)(jax.random.split(local_key, NQB)).astype(jnp.int32)
    near_blocks = groups_of[:, None] * QB_DEV + (inner_index[:, None] + near_steps) % QB_DEV
    listed = jnp.concatenate([row_ids[:, None], near_blocks, far_blocks], axis=1)
    column_order = jax.vmap(lambda sub_key: jax.random.permutation(sub_key, K_SEL))(jax.random.split(order_key, NQB)).astype(jnp.int32)
    return jnp.take_along_axis(listed, column_order, axis=1).astype(jnp.int32)


def strengthened(values, stream_key, source, target, blocks, factor):
    def block_of(dim):
        return (jnp.arange(values.shape[dim]) // (values.shape[dim] // blocks)).reshape((-1,) + (1,) * (values.ndim - 1 - dim))

    one_side = jax.random.permutation(stream_key, blocks)[block_of(target)]
    other_side = (block_of(target) + blocks // 2) % blocks
    return jnp.where((block_of(source) == one_side) | (block_of(source) == other_side), factor * values, values)


def shard_levels(own_key, dims, cuts, low, largest):
    def one(dim, shards_of):
        heights = jax.random.uniform(jax.random.fold_in(jax.random.fold_in(own_key, 6), dim), (shards_of,), jnp.float32, low / len(cuts), largest / len(cuts))
        return jnp.repeat(jnp.exp(heights), dims[dim] // shards_of).reshape((-1,) + (1,) * (len(dims) - dim - 1))

    level = one(*cuts[0])
    for cut in cuts[1:]:
        level = level * one(*cut)
    return level


def normal_values(stream_key, shape, width, reach, cuts=(), kind=jnp.bfloat16):
    gain = shard_levels(stream_key, shape, cuts, -0.22, 0.18) if cuts else 1.0
    values = jax.random.normal(stream_key, shape, jnp.float32) * width * gain
    return jnp.minimum(jnp.maximum(values, -reach), reach).astype(kind)


def gaussian_with(key, extent, scale, limit, pieces, heavy, kind=jnp.bfloat16):
    values = scale * jax.random.normal(key, extent, jnp.float32)
    if pieces:
        values = values * shard_levels(key, extent, pieces, -0.22, 0.18)
    return jnp.clip(strengthened(values, jax.random.fold_in(key, 3), *heavy), -limit, limit).astype(kind)


def setup_inputs(seed: int = 0) -> dict:
    key_of = jax.random.split(jax.random.key(seed), 7)
    return {
        "queries": draw_queries(jax.random.fold_in(key_of[6], 71), 0),
        "key_states": draw_key_states(jax.random.fold_in(key_of[6], 71), 0),
        "value_states": normal_values(key_of[2], (CELLS, HEADS * HD), 1.0, 6.0, ((0, 8), (1, 4))),
        "block_lists": draw_block_lists(jax.random.fold_in(key_of[6], 71), 0),
        "out_weight": gaussian_with(key_of[4], (HEADS * HD, D), (HEADS * HD) ** -0.5, 0.15625, ((0, 4),), (0, 1, 4, 2.0)),
        "out_grad": normal_values(key_of[5], (CELLS, D), 1.0, 6.0, ((0, 8), (1, 4))),
    }


def log_total(scores):
    row_top = lax.optimization_barrier(jnp.max(scores, axis=-1, keepdims=True))
    return row_top + jnp.log(lax.optimization_barrier(jnp.sum(jnp.exp(scores - row_top), axis=-1, keepdims=True)))

def settle(values):
    return lax.optimization_barrier(values.astype(jnp.bfloat16)).astype(jnp.float32)

def reference(queries, key_states, value_states, block_lists, out_weight, out_grad):
    score_scale = 1.0 / math.sqrt(HD)
    feature_width = HEADS * HD
    grad_attn = jnp.dot(out_grad, out_weight.T, preferred_element_type=jnp.float32).astype(jnp.bfloat16)
    key_blocks = key_states.reshape(NQB, BLK, HEADS, HD)
    value_blocks = value_states.reshape(NQB, BLK, HEADS, HD)
    query_groups = queries.reshape(GROUPS, QB_DEV, BLK, HEADS, HD)
    grad_groups = grad_attn.reshape(GROUPS, QB_DEV, BLK, HEADS, HD)
    list_groups = block_lists.reshape(GROUPS, QB_DEV, K_SEL)
    block_owner = jnp.arange(NQB, dtype=jnp.int32) // QB_DEV
    entry_order = jnp.arange(QB_DEV * K_SEL, dtype=jnp.int32)

    def group_step(grad_total, inputs):
        group_index, query_rows, grad_rows, group_lists = inputs
        key_rows = key_blocks[group_lists].reshape(QB_DEV, K_SEL * BLK, HEADS, HD).astype(jnp.float32)
        value_rows = value_blocks[group_lists].reshape(QB_DEV, K_SEL * BLK, HEADS, HD).astype(jnp.float32)
        query_f = query_rows.astype(jnp.float32)
        grad_f = grad_rows.astype(jnp.float32)
        scores = jnp.einsum('bihd,bjhd->bhij', query_f, key_rows) * score_scale
        probs = jnp.exp(scores - log_total(scores))
        probs_low = settle(probs)
        attention = jnp.einsum('bhij,bjhd->bihd', probs_low, value_rows).astype(jnp.bfloat16)
        row_delta = jnp.einsum('bihd,bihd->bhi', grad_f, attention.astype(jnp.float32))[..., None]
        value_terms = jnp.einsum('bhij,bihd->bjhd', probs_low, grad_f)
        grad_prob = jnp.einsum('bihd,bjhd->bhij', grad_f, value_rows)
        grad_score = settle(probs * (grad_prob - row_delta))
        query_grad = (jnp.einsum('bhij,bjhd->bihd', grad_score, key_rows) * score_scale).astype(jnp.bfloat16)
        key_terms = jnp.einsum('bhij,bihd->bjhd', grad_score, query_f) * score_scale
        slot_terms = jnp.concatenate([key_terms.reshape(QB_DEV * K_SEL, BLK, feature_width), value_terms.reshape(QB_DEV * K_SEL, BLK, feature_width)], axis=2)
        flat_ids = group_lists.reshape(-1).astype(jnp.int32)
        same_block = flat_ids[:, None] == flat_ids[None, :]
        first_seen = jnp.logical_not(jnp.any(same_block & (entry_order[None, :] < entry_order[:, None]), axis=1))
        block_sums = jnp.zeros((NQB, BLK, 2 * feature_width), jnp.float32).at[flat_ids].add(slot_terms)
        grouped = block_sums[flat_ids]
        own_group = (block_owner[flat_ids] == group_index)[:, None, None]
        settled = jnp.where(own_group, grouped, settle(grouped))
        settled = jnp.where(first_seen[:, None, None], settled, jnp.zeros_like(settled))
        return (grad_total.at[flat_ids].add(settled), (attention, query_grad))
    zero_carry = jnp.zeros((NQB, BLK, 2 * feature_width), jnp.float32)
    grad_total, (attention, query_grad) = lax.scan(group_step, zero_carry, (jnp.arange(GROUPS, dtype=jnp.int32), query_groups, grad_groups, list_groups))
    attention = attention.reshape(CELLS, feature_width)
    part_width = feature_width // N_HEAD
    mixed_sum = jnp.zeros((CELLS, D), jnp.float32)
    for part_index in range(N_HEAD):
        low_edge = part_index * part_width
        part_product = jnp.dot(attention[:, low_edge:low_edge + part_width], out_weight[low_edge:low_edge + part_width], preferred_element_type=jnp.float32)
        mixed_sum = mixed_sum + settle(part_product)
    grad_total = grad_total.reshape(CELLS, 2 * feature_width)
    return (mixed_sum.astype(jnp.bfloat16), query_grad.reshape(CELLS, feature_width), grad_total[:, :feature_width].astype(jnp.bfloat16), grad_total[:, feature_width:].astype(jnp.bfloat16))
```

```python
import functools
import math

import jax
import jax.numpy as jnp
from jax import lax
from jax.experimental import pallas as pl
from jax.experimental.pallas import tpu as pltpu
from jax.sharding import PartitionSpec as P

HD = 128
BLK = 128
K_SEL = 4
MESH = pl.DeviceIdType.MESH
BF = jnp.bfloat16
F32 = jnp.float32


def dot_nn(a, b):
    return lax.dot_general(a, b, (((1,), (0,)), ((), ())), preferred_element_type=F32)


def dot_nt(a, b):
    return lax.dot_general(a, b, (((1,), (1,)), ((), ())), preferred_element_type=F32)


def dot_tn(a, b):
    return lax.dot_general(a, b, (((0,), (0,)), ((), ())), preferred_element_type=F32)


def kernel(
    n_seq, n_head, lists, q, k, v, og, w_hbm,
    att_o, dq_o, dk_o, dv_o,
    table, kv_send, w, og_all, p_scr, ds_scr, attn, part_send, part_recv,
    ga_acc, ga, ret_send, ret_recv, acc_k, acc_v, slot_s, asked_s, idx_s,
    w_sem, og_up, og_down, og_recv, kv_ssem, kv_rsem, pt_ssem, pt_rsem, rt_ssem, rt_rsem,
):
    cells, width = q.shape
    blocks = cells // BLK
    heads = width // HD
    scale = 1.0 / math.sqrt(HD)
    s_me = lax.axis_index("seq")
    z = lax.axis_index("head")

    w_copy = pltpu.make_async_copy(w_hbm, w, w_sem)
    w_copy.start()

    barrier = pltpu.get_barrier_semaphore()
    for o in range(1, n_head):
        pl.semaphore_signal(
            barrier, inc=1, device_id={"head": lax.rem(z + o, n_head)}, device_id_type=MESH
        )
    for o in range(1, n_seq):
        pl.semaphore_signal(
            barrier, inc=1, device_id={"seq": lax.rem(s_me + o, n_seq)}, device_id_type=MESH
        )
    pl.semaphore_wait(barrier, n_head - 1 + n_seq - 1)

    def og_copy(shard, up, own):
        src = og if own else og_all.at[shard]
        return pltpu.make_async_remote_copy(
            src_ref=src,
            dst_ref=og_all.at[shard],
            send_sem=(og_up if up else og_down).at[shard],
            recv_sem=og_recv.at[shard],
            device_id={"head": z + 1 if up else z - 1},
            device_id_type=MESH,
        )

    @pl.when(z < n_head - 1)
    def _():
        og_copy(z, True, True).start()

    @pl.when(z > 0)
    def _():
        og_copy(z, False, True).start()

    def kv_copy(d):
        return pltpu.make_async_remote_copy(
            src_ref=kv_send.at[d],
            dst_ref=table.at[s_me],
            send_sem=kv_ssem.at[d],
            recv_sem=kv_rsem.at[s_me],
            device_id={"seq": d},
            device_id_type=MESH,
        )

    def kv_start(i, carry):
        d = lax.rem(s_me + n_seq - i, n_seq)
        asked = jnp.int32(0)
        for r in range(blocks):
            for c in range(K_SEL):
                entry = lists[d * blocks + r, c] - s_me * blocks
                asked = jnp.where((entry >= 0) & (entry < blocks), entry, asked)
        asked_s[d] = asked
        kv_send[d, :, :width] = k[asked]
        kv_send[d, :, width:] = v[asked]
        kv_copy(d).start()
        return carry

    lax.fori_loop(1, n_seq, kv_start, 0)

    for b in range(blocks):
        table[n_seq + b, :, :width] = k[b]
        table[n_seq + b, :, width:] = v[b]
        for c in range(K_SEL):
            entry = lists[s_me * blocks + b, c]
            near = entry - s_me * blocks
            own = (near >= 0) & (near < blocks)
            slot_s[b * K_SEL + c] = jnp.where(own, n_seq + near, lax.div(entry, jnp.int32(blocks)))
        ds_scr[b, K_SEL] = jnp.zeros((BLK, BLK), BF)
        for h in range(heads):
            p_scr[h, b, K_SEL] = jnp.zeros((BLK, BLK), BF)

    def fill_index(t, carry):
        for b in range(blocks):
            place = jnp.int32(K_SEL)
            for c in range(K_SEL):
                place = jnp.where(slot_s[b * K_SEL + c] == t, c, place)
            idx_s[t * blocks + b] = place
        return carry

    lax.fori_loop(0, n_seq + blocks, fill_index, 0)

    w_copy.wait()

    def w_cols(shard):
        return w[:, pl.ds(pl.multiple_of(shard * width, width), width)]

    ga_acc[...] = dot_nt(og[...], w_cols(z))

    def og_round(j, carry):
        step = j // 2 + 1
        up = lax.rem(j, 2) == 0
        shard = z + step * (2 * lax.rem(j, 2) - 1)

        @pl.when((shard >= 0) & (shard < n_head))
        def _():
            og_copy(shard, True, False).wait_recv()

            @pl.when(up & (z < n_head - 1))
            def _():
                og_copy(shard, True, False).start()

            @pl.when((lax.rem(j, 2) == 1) & (z > 0))
            def _():
                og_copy(shard, False, False).start()

            ga_acc[...] += dot_nt(og_all[shard], w_cols(shard))

        return carry

    lax.fori_loop(0, 2 * (n_head - 2), og_round, 0)

    def kv_wait(i, carry):
        src = lax.rem(s_me + i, n_seq)
        pltpu.make_async_remote_copy(
            src_ref=kv_send.at[src],
            dst_ref=table.at[src],
            send_sem=kv_ssem.at[src],
            recv_sem=kv_rsem.at[src],
            device_id={"seq": src},
            device_id_type=MESH,
        ).wait_recv()
        return carry

    lax.fori_loop(1, n_seq, kv_wait, 0)

    def picked(b, offset):
        cols = pl.ds(pl.multiple_of(offset, HD), HD)
        return jnp.concatenate(
            [table[slot_s[b * K_SEL + c], :, cols] for c in range(K_SEL)], axis=0
        )

    def forward(h, carry):
        cols = pl.ds(pl.multiple_of(h * HD, HD), HD)
        for b in range(blocks):
            rows = slice(b * BLK, (b + 1) * BLK)
            scores = dot_nt(picked(b, h * HD), q[rows, cols]) * scale
            top = jnp.max(scores, axis=0, keepdims=True)
            weights = jnp.exp(scores - top)
            total = jnp.sum(weights, axis=0, keepdims=True)
            probs = (weights * (1.0 / total)).astype(BF)
            for c in range(K_SEL):
                p_scr[h, b, c] = probs[c * BLK:(c + 1) * BLK]
            attn[rows, cols] = dot_tn(probs, picked(b, width + h * HD)).astype(BF)
        return carry

    lax.fori_loop(0, heads, forward, 0)

    def part_copy(d):
        return pltpu.make_async_remote_copy(
            src_ref=part_send.at[d],
            dst_ref=part_recv.at[z],
            send_sem=pt_ssem.at[d],
            recv_sem=pt_rsem.at[z],
            device_id={"head": d},
            device_id_type=MESH,
        )

    def project(i, carry):
        d = lax.rem(z + i, n_head)
        part_send[d] = dot_nn(attn[...], w_cols(d)).astype(BF)

        @pl.when(i < n_head)
        def _():
            part_copy(d).start()

        return carry

    lax.fori_loop(1, n_head + 1, project, 0)

    lax.fori_loop(2 * (n_head - 2), 2 * (n_head - 1), og_round, 0)
    ga[...] = ga_acc[...].astype(BF)

    def ret_copy(h, d):
        return pltpu.make_async_remote_copy(
            src_ref=ret_send.at[h, d],
            dst_ref=ret_recv.at[h, s_me],
            send_sem=rt_ssem.at[h, d],
            recv_sem=rt_rsem.at[h, s_me],
            device_id={"seq": d},
            device_id_type=MESH,
        )

    def backward(h, carry):
        cols = pl.ds(pl.multiple_of(h * HD, HD), HD)
        for b in range(blocks):
            rows = slice(b * BLK, (b + 1) * BLK)
            probs = jnp.concatenate(
                [p_scr[h, b, c] for c in range(K_SEL)], axis=0
            ).astype(F32)
            grad_prob = dot_nt(picked(b, width + h * HD), ga[rows, cols])
            delta = jnp.sum(probs * grad_prob, axis=0, keepdims=True)
            grad_score = (probs * (grad_prob - delta)).astype(BF)
            for c in range(K_SEL):
                ds_scr[b, c] = grad_score[c * BLK:(c + 1) * BLK]
            dq_o[rows, cols] = (dot_tn(grad_score, picked(b, h * HD)) * scale).astype(BF)
        q_cols = q[:, cols]
        g_cols = ga[:, cols]

        def terms(t):
            places = [idx_s[t * blocks + b] for b in range(blocks)]
            ds_t = jnp.concatenate([ds_scr[b, places[b]] for b in range(blocks)], axis=1)
            p_t = jnp.concatenate([p_scr[h, b, places[b]] for b in range(blocks)], axis=1)
            return dot_nn(ds_t, q_cols) * scale, dot_nn(p_t, g_cols)

        for i in range(1, n_seq):
            d = lax.rem(s_me + n_seq - i, n_seq)
            key_part, value_part = terms(d)
            ret_send[h, d, :, :HD] = key_part.astype(BF)
            ret_send[h, d, :, HD:] = value_part.astype(BF)
            ret_copy(h, d).start()
        for b in range(blocks):
            rows = slice(b * BLK, (b + 1) * BLK)
            acc_k[rows, cols], acc_v[rows, cols] = terms(n_seq + b)
        return carry

    lax.fori_loop(0, heads, backward, 0)

    for i in range(1, n_head):
        d = lax.rem(z + i, n_head)
        pltpu.make_async_remote_copy(
            src_ref=part_send.at[d],
            dst_ref=part_recv.at[d],
            send_sem=pt_ssem.at[d],
            recv_sem=pt_rsem.at[d],
            device_id={"head": d},
            device_id_type=MESH,
        ).wait_recv()

    for b in range(blocks):
        rows = slice(b * BLK, (b + 1) * BLK)
        total = part_send[z, rows, :].astype(F32)
        for i in range(1, n_head):
            total += part_recv[lax.rem(z + i, n_head), rows, :].astype(F32)
        att_o[rows, :] = total.astype(BF)

    def collect(h, carry):
        cols = pl.ds(pl.multiple_of(h * HD, HD), HD)

        def ret_wait(i, inner):
            src = lax.rem(s_me + i, n_seq)
            pltpu.make_async_remote_copy(
                src_ref=ret_send.at[h, src],
                dst_ref=ret_recv.at[h, src],
                send_sem=rt_ssem.at[h, src],
                recv_sem=rt_rsem.at[h, src],
                device_id={"seq": src},
                device_id_type=MESH,
            ).wait_recv()
            return inner

        lax.fori_loop(1, n_seq, ret_wait, 0)
        for b in range(blocks):
            rows = slice(b * BLK, (b + 1) * BLK)
            key_sum = acc_k[rows, cols]
            value_sum = acc_v[rows, cols]
            for i in range(1, n_seq):
                src = lax.rem(s_me + i, n_seq)
                flag = jnp.where(asked_s[src] == b, 1.0, 0.0)
                key_sum += flag * ret_recv[h, src, :, :HD].astype(F32)
                value_sum += flag * ret_recv[h, src, :, HD:].astype(F32)
            dk_o[rows, cols] = key_sum.astype(BF)
            dv_o[rows, cols] = value_sum.astype(BF)
        return carry

    lax.fori_loop(0, heads, collect, 0)

    @pl.when(z < n_head - 1)
    def _():
        og_copy(z, True, True).wait_send()

    @pl.when(z > 0)
    def _():
        og_copy(z, False, True).wait_send()

    for step in range(1, n_head - 1):
        @pl.when((z - step >= 0) & (z < n_head - 1))
        def _():
            og_copy(z - step, True, False).wait_send()

        @pl.when((z + step < n_head) & (z > 0))
        def _():
            og_copy(z + step, False, False).wait_send()

    def seq_drain(i, carry):
        d = lax.rem(s_me + i, n_seq)
        kv_copy(d).wait_send()

        def one(h, inner):
            ret_copy(h, d).wait_send()
            return inner

        return lax.fori_loop(0, heads, one, carry)

    lax.fori_loop(1, n_seq, seq_drain, 0)
    for i in range(1, n_head):
        part_copy(lax.rem(z + i, n_head)).wait_send()


def local(queries, key_states, value_states, block_lists, out_weight, out_grad):
    n_seq = lax.axis_size("seq")
    n_head = lax.axis_size("head")
    cells, width = queries.shape
    blocks = cells // BLK
    heads = width // HD
    slots = n_seq + blocks
    vmem = pl.BlockSpec(memory_space=pltpu.VMEM)
    sem = pltpu.SemaphoreType.DMA
    out = jax.ShapeDtypeStruct((cells, width), BF)
    return pl.pallas_call(
        functools.partial(kernel, n_seq, n_head),
        out_shape=(out, out, out, out),
        in_specs=[
            pl.BlockSpec(memory_space=pltpu.SMEM), vmem, vmem, vmem, vmem,
            pl.BlockSpec(memory_space=pl.ANY),
        ],
        out_specs=(vmem, vmem, vmem, vmem),
        scratch_shapes=[
            pltpu.VMEM((slots, BLK, 2 * width), BF),
            pltpu.VMEM((n_seq, BLK, 2 * width), BF),
            pltpu.VMEM(out_weight.shape, BF),
            pltpu.VMEM((n_head, cells, width), BF),
            pltpu.VMEM((heads, blocks, K_SEL + 1, BLK, BLK), BF),
            pltpu.VMEM((blocks, K_SEL + 1, BLK, BLK), BF),
            pltpu.VMEM((cells, width), BF),
            pltpu.VMEM((n_head, cells, width), BF),
            pltpu.VMEM((n_head, cells, width), BF),
            pltpu.VMEM((cells, width), F32),
            pltpu.VMEM((cells, width), BF),
            pltpu.VMEM((heads, n_seq, BLK, 2 * HD), BF),
            pltpu.VMEM((heads, n_seq, BLK, 2 * HD), BF),
            pltpu.VMEM((cells, width), F32),
            pltpu.VMEM((cells, width), F32),
            pltpu.SMEM((blocks * K_SEL,), jnp.int32),
            pltpu.SMEM((n_seq,), jnp.int32),
            pltpu.SMEM((slots * blocks,), jnp.int32),
            sem, sem((n_head,)), sem((n_head,)), sem((n_head,)),
            sem((n_seq,)), sem((n_seq,)), sem((n_head,)), sem((n_head,)),
            sem((heads, n_seq)), sem((heads, n_seq)),
        ],
        compiler_params=pltpu.CompilerParams(
            collective_id=0, has_side_effects=True, vmem_limit_bytes=60 * 1024 * 1024
        ),
        cost_estimate=pl.CostEstimate(
            flops=8 * 10**9, bytes_accessed=20 * 10**6, transcendentals=10**6
        ),
    )(
        block_lists,
        queries,
        key_states.reshape(blocks, BLK, width),
        value_states.reshape(blocks, BLK, width),
        out_grad,
        out_weight,
    )


def solution(mesh):
    in_specs = (
        P("seq", "head"),
        P("seq", "head"),
        P("seq", "head"),
        P(),
        P("head", None),
        P("seq", "head"),
    )
    out_specs = (P("seq", "head"), P("seq", "head"), P("seq", "head"), P("seq", "head"))
    return jax.shard_map(local, mesh=mesh, in_specs=in_specs, out_specs=out_specs, check_vma=False)
```

```python
import functools
import math

import jax
import jax.numpy as jnp
from jax import lax
from jax.experimental import pallas as pl
from jax.experimental.pallas import tpu as pltpu
from jax.sharding import PartitionSpec as P

HD = 128
BLK = 128
K_SEL = 4
MESH = pl.DeviceIdType.MESH
BF = jnp.bfloat16
F32 = jnp.float32


def dot_nn(a, b):
    return lax.dot_general(a, b, (((1,), (0,)), ((), ())), preferred_element_type=F32)


def dot_nt(a, b):
    return lax.dot_general(a, b, (((1,), (1,)), ((), ())), preferred_element_type=F32)


def dot_tn(a, b):
    return lax.dot_general(a, b, (((0,), (0,)), ((), ())), preferred_element_type=F32)


def kernel(
    n_seq, n_head, lists_hbm, q, k, v, og, w_hbm,
    att_o, dq_o, dk_o, dv_o,
    table, kv_send, w, og_all, p_scr, ds_scr, attn, part_send, from_below, from_above,
    ga_acc, ga, ret_send, ret_recv, acc_k, acc_v, lists, slot_s, asked_s, idx_s,
    lists_sem, w_sem, og_up, og_down, og_recv, kv_ssem, kv_rsem,
    pt_ssem, below_sem, above_sem, rt_ssem, rt_rsem,
):
    cells, width = q.shape
    blocks = cells // BLK
    heads = width // HD
    scale = 1.0 / math.sqrt(HD)
    s_me = lax.axis_index("seq")
    z = lax.axis_index("head")

    w_copy = pltpu.make_async_copy(w_hbm, w, w_sem)
    w_copy.start()
    lists_copy = pltpu.make_async_copy(lists_hbm, lists, lists_sem)
    lists_copy.start()

    barrier = pltpu.get_barrier_semaphore()
    for o in range(1, n_head):
        pl.semaphore_signal(
            barrier, inc=1, device_id={"head": lax.rem(z + o, n_head)}, device_id_type=MESH
        )
    for o in range(1, n_seq):
        pl.semaphore_signal(
            barrier, inc=1, device_id={"seq": lax.rem(s_me + o, n_seq)}, device_id_type=MESH
        )
    pl.semaphore_wait(barrier, n_head - 1 + n_seq - 1)

    def chunk(c):
        return pl.ds(pl.multiple_of(c * BLK, BLK), BLK)

    def og_copy(shard, c, up, own):
        src = og.at[chunk(c), :] if own else og_all.at[shard, chunk(c), :]
        return pltpu.make_async_remote_copy(
            src_ref=src,
            dst_ref=og_all.at[shard, chunk(c), :],
            send_sem=(og_up if up else og_down).at[shard, c],
            recv_sem=og_recv.at[shard, c],
            device_id={"head": z + 1 if up else z - 1},
            device_id_type=MESH,
        )

    for c in range(blocks):
        @pl.when(z < n_head - 1)
        def _():
            og_copy(z, c, True, True).start()

        @pl.when(z > 0)
        def _():
            og_copy(z, c, False, True).start()

    lists_copy.wait()

    def kv_copy(d):
        return pltpu.make_async_remote_copy(
            src_ref=kv_send.at[d],
            dst_ref=table.at[s_me],
            send_sem=kv_ssem.at[d],
            recv_sem=kv_rsem.at[s_me],
            device_id={"seq": d},
            device_id_type=MESH,
        )

    def kv_start(i, carry):
        d = lax.rem(s_me + n_seq - i, n_seq)
        asked = jnp.int32(0)
        for r in range(blocks):
            for c in range(K_SEL):
                entry = lists[c, d * blocks + r] - s_me * blocks
                asked = jnp.where((entry >= 0) & (entry < blocks), entry, asked)
        asked_s[d] = asked
        kv_send[d, :, :width] = k[asked]
        kv_send[d, :, width:] = v[asked]
        kv_copy(d).start()
        return carry

    lax.fori_loop(1, n_seq, kv_start, 0)

    for b in range(blocks):
        table[n_seq + b, :, :width] = k[b]
        table[n_seq + b, :, width:] = v[b]
        for c in range(K_SEL):
            entry = lists[c, s_me * blocks + b]
            near = entry - s_me * blocks
            own = (near >= 0) & (near < blocks)
            slot_s[b * K_SEL + c] = jnp.where(own, n_seq + near, lax.div(entry, jnp.int32(blocks)))
        ds_scr[b, K_SEL] = jnp.zeros((BLK, BLK), BF)
        for h in range(heads):
            p_scr[h, b, K_SEL] = jnp.zeros((BLK, BLK), BF)

    def fill_index(t, carry):
        for b in range(blocks):
            place = jnp.int32(K_SEL)
            for c in range(K_SEL):
                place = jnp.where(slot_s[b * K_SEL + c] == t, c, place)
            idx_s[t * blocks + b] = place
        return carry

    lax.fori_loop(0, n_seq + blocks, fill_index, 0)

    w_copy.wait()

    def w_cols(shard):
        return w[:, pl.ds(pl.multiple_of(shard * width, width), width)]

    ga_acc[...] = dot_nt(og[...], w_cols(z))

    def og_round(step, carry):
        def one(c, inner):
            @pl.when(z - step >= 0)
            def _():
                og_copy(z - step, c, True, False).wait_recv()

                @pl.when(z < n_head - 1)
                def _():
                    og_copy(z - step, c, True, False).start()

            @pl.when(z + step < n_head)
            def _():
                og_copy(z + step, c, False, False).wait_recv()

                @pl.when(z > 0)
                def _():
                    og_copy(z + step, c, False, False).start()

            return inner

        lax.fori_loop(0, blocks, one, 0)

        @pl.when(z - step >= 0)
        def _():
            ga_acc[...] += dot_nt(og_all[z - step], w_cols(z - step))

        @pl.when(z + step < n_head)
        def _():
            ga_acc[...] += dot_nt(og_all[z + step], w_cols(z + step))

        return carry

    lax.fori_loop(1, n_head - 1, og_round, 0)

    def kv_wait(i, carry):
        src = lax.rem(s_me + i, n_seq)
        pltpu.make_async_remote_copy(
            src_ref=kv_send.at[src],
            dst_ref=table.at[src],
            send_sem=kv_ssem.at[src],
            recv_sem=kv_rsem.at[src],
            device_id={"seq": src},
            device_id_type=MESH,
        ).wait_recv()
        return carry

    lax.fori_loop(1, n_seq, kv_wait, 0)

    def picked(b, offset):
        cols = pl.ds(pl.multiple_of(offset, HD), HD)
        return jnp.concatenate(
            [table[slot_s[b * K_SEL + c], :, cols] for c in range(K_SEL)], axis=0
        )

    def forward(h, carry):
        cols = pl.ds(pl.multiple_of(h * HD, HD), HD)
        for b in range(blocks):
            rows = slice(b * BLK, (b + 1) * BLK)
            scores = dot_nt(picked(b, h * HD), q[rows, cols]) * scale
            top = jnp.max(scores, axis=0, keepdims=True)
            weights = jnp.exp(scores - top)
            total = jnp.sum(weights, axis=0, keepdims=True)
            probs = (weights * (1.0 / total)).astype(BF)
            for c in range(K_SEL):
                p_scr[h, b, c] = probs[c * BLK:(c + 1) * BLK]
            attn[rows, cols] = dot_tn(probs, picked(b, width + h * HD)).astype(BF)
        return carry

    lax.fori_loop(0, heads, forward, 0)

    def part_copy(d, c, up):
        landing = from_below if up else from_above
        return pltpu.make_async_remote_copy(
            src_ref=part_send.at[d, chunk(c), :],
            dst_ref=landing.at[d, chunk(c), :],
            send_sem=pt_ssem.at[d, c],
            recv_sem=(below_sem if up else above_sem).at[d, c],
            device_id={"head": z + 1 if up else z - 1},
            device_id_type=MESH,
        )

    def project(i, carry):
        last = lax.div(z, n_head - 1)
        d = last * i + (1 - last) * (n_head - 1 - i)
        part_send[d] = dot_nn(attn[...], w_cols(d)).astype(BF)
        for c in range(blocks):
            @pl.when((z == 0) & (d > 0))
            def _():
                part_copy(d, c, True).start()

            @pl.when((z == n_head - 1) & (d < n_head - 1))
            def _():
                part_copy(d, c, False).start()

        return carry

    lax.fori_loop(0, n_head, project, 0)

    og_round(n_head - 1, 0)
    ga[...] = ga_acc[...].astype(BF)

    def ret_copy(h, d):
        return pltpu.make_async_remote_copy(
            src_ref=ret_send.at[h, d],
            dst_ref=ret_recv.at[h, s_me],
            send_sem=rt_ssem.at[h, d],
            recv_sem=rt_rsem.at[h, s_me],
            device_id={"seq": d},
            device_id_type=MESH,
        )

    def backward(h, carry):
        cols = pl.ds(pl.multiple_of(h * HD, HD), HD)
        for b in range(blocks):
            rows = slice(b * BLK, (b + 1) * BLK)
            probs = jnp.concatenate(
                [p_scr[h, b, c] for c in range(K_SEL)], axis=0
            ).astype(F32)
            grad_prob = dot_nt(picked(b, width + h * HD), ga[rows, cols])
            delta = jnp.sum(probs * grad_prob, axis=0, keepdims=True)
            grad_score = (probs * (grad_prob - delta)).astype(BF)
            for c in range(K_SEL):
                ds_scr[b, c] = grad_score[c * BLK:(c + 1) * BLK]
            dq_o[rows, cols] = (dot_tn(grad_score, picked(b, h * HD)) * scale).astype(BF)
        q_cols = q[:, cols]
        g_cols = ga[:, cols]

        def terms(t):
            places = [idx_s[t * blocks + b] for b in range(blocks)]
            ds_t = jnp.concatenate([ds_scr[b, places[b]] for b in range(blocks)], axis=1)
            p_t = jnp.concatenate([p_scr[h, b, places[b]] for b in range(blocks)], axis=1)
            return dot_nn(ds_t, q_cols) * scale, dot_nn(p_t, g_cols)

        for i in range(1, n_seq):
            d = lax.rem(s_me + n_seq - i, n_seq)
            key_part, value_part = terms(d)
            ret_send[h, d, :, :HD] = key_part.astype(BF)
            ret_send[h, d, :, HD:] = value_part.astype(BF)
            ret_copy(h, d).start()
        for b in range(blocks):
            rows = slice(b * BLK, (b + 1) * BLK)
            acc_k[rows, cols], acc_v[rows, cols] = terms(n_seq + b)
        return carry

    lax.fori_loop(0, heads, backward, 0)

    def hand_on(tick, carry):
        u = tick - z

        @pl.when((z > 0) & (u >= 0) & (u < blocks * (n_head - 1 - z)))
        def _():
            d = n_head - 1 - u // blocks
            c = lax.rem(u, blocks)
            part_copy(d, c, True).wait_recv()
            part_send[d, chunk(c), :] = (
                part_send[d, chunk(c), :].astype(F32) + from_below[d, chunk(c), :].astype(F32)
            ).astype(BF)
            part_copy(d, c, True).start()

        t = tick - (n_head - 1 - z)

        @pl.when((z < n_head - 1) & (t >= 0) & (t < blocks * z))
        def _():
            d = t // blocks
            c = lax.rem(t, blocks)
            part_copy(d, c, False).wait_recv()
            part_send[d, chunk(c), :] = (
                part_send[d, chunk(c), :].astype(F32) + from_above[d, chunk(c), :].astype(F32)
            ).astype(BF)
            part_copy(d, c, False).start()

        return carry

    lax.fori_loop(1, blocks * (n_head - 1) + n_head, hand_on, 0)

    def collect(h, carry):
        cols = pl.ds(pl.multiple_of(h * HD, HD), HD)

        def ret_wait(i, inner):
            src = lax.rem(s_me + i, n_seq)
            pltpu.make_async_remote_copy(
                src_ref=ret_send.at[h, src],
                dst_ref=ret_recv.at[h, src],
                send_sem=rt_ssem.at[h, src],
                recv_sem=rt_rsem.at[h, src],
                device_id={"seq": src},
                device_id_type=MESH,
            ).wait_recv()
            return inner

        lax.fori_loop(1, n_seq, ret_wait, 0)
        for b in range(blocks):
            rows = slice(b * BLK, (b + 1) * BLK)
            key_sum = acc_k[rows, cols]
            value_sum = acc_v[rows, cols]
            for i in range(1, n_seq):
                src = lax.rem(s_me + i, n_seq)
                flag = jnp.where(asked_s[src] == b, 1.0, 0.0)
                key_sum += flag * ret_recv[h, src, :, :HD].astype(F32)
                value_sum += flag * ret_recv[h, src, :, HD:].astype(F32)
            dk_o[rows, cols] = key_sum.astype(BF)
            dv_o[rows, cols] = value_sum.astype(BF)
        return carry

    lax.fori_loop(0, heads, collect, 0)

    for c in range(blocks):
        rows = slice(c * BLK, (c + 1) * BLK)
        ga_acc[rows, :] = part_send[z, rows, :].astype(F32)

        @pl.when(z > 0)
        def _():
            part_copy(z, c, True).wait_recv()
            ga_acc[rows, :] += from_below[z, rows, :].astype(F32)

        @pl.when(z < n_head - 1)
        def _():
            part_copy(z, c, False).wait_recv()
            ga_acc[rows, :] += from_above[z, rows, :].astype(F32)

        att_o[rows, :] = ga_acc[rows, :].astype(BF)

    def og_drain(c, carry):
        for step in range(n_head - 1):
            @pl.when((z - step >= 0) & (z < n_head - 1))
            def _():
                og_copy(z - step, c, True, False).wait_send()

            @pl.when((z + step < n_head) & (z > 0))
            def _():
                og_copy(z + step, c, False, False).wait_send()

        for d in range(n_head):
            @pl.when(z != d)
            def _():
                part_copy(d, c, True).wait_send()

        return carry

    lax.fori_loop(0, blocks, og_drain, 0)

    def seq_drain(i, carry):
        d = lax.rem(s_me + i, n_seq)
        kv_copy(d).wait_send()

        def one(h, inner):
            ret_copy(h, d).wait_send()
            return inner

        return lax.fori_loop(0, heads, one, carry)

    lax.fori_loop(1, n_seq, seq_drain, 0)


def write_out(a0, a1, a2, a3, o0, o1, o2, o3, sems):
    copies = [
        pltpu.make_async_copy(src, dst, sems.at[i])
        for i, (src, dst) in enumerate(((a0, o0), (a1, o1), (a2, o2), (a3, o3)))
    ]
    for copy in copies:
        copy.start()
    for copy in copies:
        copy.wait()


def local(queries, key_states, value_states, block_lists, out_weight, out_grad):
    n_seq = lax.axis_size("seq")
    n_head = lax.axis_size("head")
    cells, width = queries.shape
    blocks = cells // BLK
    heads = width // HD
    slots = n_seq + blocks
    vmem = pl.BlockSpec(memory_space=pltpu.VMEM)
    hbm = pl.BlockSpec(memory_space=pl.ANY)
    sem = pltpu.SemaphoreType.DMA
    out = jax.ShapeDtypeStruct((cells, width), BF)
    held = pltpu.VMEM((cells, width), BF)
    results = pl.pallas_call(
        functools.partial(kernel, n_seq, n_head),
        out_shape=(held, held, held, held),
        in_specs=[
            hbm, vmem, vmem, vmem, vmem, hbm,
        ],
        out_specs=(vmem, vmem, vmem, vmem),
        scratch_shapes=[
            pltpu.VMEM((slots, BLK, 2 * width), BF),
            pltpu.VMEM((n_seq, BLK, 2 * width), BF),
            pltpu.VMEM(out_weight.shape, BF),
            pltpu.VMEM((n_head, cells, width), BF),
            pltpu.VMEM((heads, blocks, K_SEL + 1, BLK, BLK), BF),
            pltpu.VMEM((blocks, K_SEL + 1, BLK, BLK), BF),
            pltpu.VMEM((cells, width), BF),
            pltpu.VMEM((n_head, cells, width), BF),
            pltpu.VMEM((n_head, cells, width), BF),
            pltpu.VMEM((n_head, cells, width), BF),
            pltpu.VMEM((cells, width), F32),
            pltpu.VMEM((cells, width), BF),
            pltpu.VMEM((heads, n_seq, BLK, 2 * HD), BF),
            pltpu.VMEM((heads, n_seq, BLK, 2 * HD), BF),
            pltpu.VMEM((cells, width), F32),
            pltpu.VMEM((cells, width), F32),
            pltpu.SMEM(block_lists.shape[::-1], jnp.int32),
            pltpu.SMEM((blocks * K_SEL,), jnp.int32),
            pltpu.SMEM((n_seq,), jnp.int32),
            pltpu.SMEM((slots * blocks,), jnp.int32),
            sem, sem, sem((n_head, blocks)), sem((n_head, blocks)), sem((n_head, blocks)),
            sem((n_seq,)), sem((n_seq,)),
            sem((n_head, blocks)), sem((n_head, blocks)), sem((n_head, blocks)),
            sem((heads, n_seq)), sem((heads, n_seq)),
        ],
        compiler_params=pltpu.CompilerParams(
            collective_id=0, has_side_effects=True, vmem_limit_bytes=56 * 1024 * 1024
        ),
        cost_estimate=pl.CostEstimate(
            flops=8 * 10**9, bytes_accessed=20 * 10**6, transcendentals=10**6
        ),
    )(
        block_lists.T,
        queries,
        key_states.reshape(blocks, BLK, width),
        value_states.reshape(blocks, BLK, width),
        out_grad,
        out_weight,
    )
    return pl.pallas_call(
        write_out,
        out_shape=(out, out, out, out),
        in_specs=[vmem] * 4,
        out_specs=(hbm,) * 4,
        scratch_shapes=[sem((4,))],
    )(*results)


def solution(mesh):
    in_specs = (
        P("seq", "head"),
        P("seq", "head"),
        P("seq", "head"),
        P(),
        P("head", None),
        P("seq", "head"),
    )
    out_specs = (P("seq", "head"), P("seq", "head"), P("seq", "head"), P("seq", "head"))
    return jax.shard_map(local, mesh=mesh, in_specs=in_specs, out_specs=out_specs, check_vma=False)
```

```python
import functools
import math

import jax
import jax.numpy as jnp
from jax import lax
from jax.experimental import pallas as pl
from jax.experimental.pallas import tpu as pltpu
from jax.sharding import PartitionSpec as P

HD = 128
BLK = 128
K_SEL = 4
MESH = pl.DeviceIdType.MESH
BF = jnp.bfloat16
F32 = jnp.float32


def dot_nn(a, b):
    return lax.dot_general(a, b, (((1,), (0,)), ((), ())), preferred_element_type=F32)


def dot_nt(a, b):
    return lax.dot_general(a, b, (((1,), (1,)), ((), ())), preferred_element_type=F32)


def dot_tn(a, b):
    return lax.dot_general(a, b, (((0,), (0,)), ((), ())), preferred_element_type=F32)


def kernel(
    n_seq, n_head, lists_hbm, q_hbm, k_hbm, v_hbm, og, w_hbm,
    att_o, dq_o, dk_o, dv_o,
    q, k, v, table_k, table_v, k_send, v_send, w, og_all, p_scr, ds_scr, attn, part_send, from_below, from_above,
    ga_acc, ga, ret_send, ret_recv, acc_k, acc_v, lists, slot_s, asked_s, idx_s,
    load_sem, og_up, og_down, og_recv, k_ssem, k_rsem, v_ssem, v_rsem,
    pt_ssem, below_sem, above_sem, rt_ssem, rt_rsem,
):
    cells, width = q.shape
    blocks = cells // BLK
    heads = width // HD
    scale = 1.0 / math.sqrt(HD)
    s_me = lax.axis_index("seq")
    z = lax.axis_index("head")

    barrier = pltpu.get_barrier_semaphore()
    for o in range(1, n_head):
        pl.semaphore_signal(
            barrier, inc=1, device_id={"head": lax.rem(z + o, n_head)}, device_id_type=MESH
        )
    for o in range(1, n_seq):
        pl.semaphore_signal(
            barrier, inc=1, device_id={"seq": lax.rem(s_me + o, n_seq)}, device_id_type=MESH
        )
    loads = [
        pltpu.make_async_copy(src, dst, load_sem.at[i])
        for i, (src, dst) in enumerate(
            ((lists_hbm, lists), (k_hbm, k), (v_hbm, v), (og, og_all.at[z]), (q_hbm, q), (w_hbm, w))
        )
    ]
    for load in loads:
        load.start()
    pl.semaphore_wait(barrier, n_head - 1 + n_seq - 1)

    def chunk(c):
        return pl.ds(pl.multiple_of(c * BLK, BLK), BLK)

    def og_copy(shard, c, up, own):
        src = og.at[chunk(c), :] if own else og_all.at[shard, chunk(c), :]
        return pltpu.make_async_remote_copy(
            src_ref=src,
            dst_ref=og_all.at[shard, chunk(c), :],
            send_sem=(og_up if up else og_down).at[shard, c],
            recv_sem=og_recv.at[shard, c],
            device_id={"head": z + 1 if up else z - 1},
            device_id_type=MESH,
        )

    for c in range(blocks):
        @pl.when(z < n_head - 1)
        def _():
            og_copy(z, c, True, True).start()

        @pl.when(z > 0)
        def _():
            og_copy(z, c, False, True).start()

    for load in loads[:3]:
        load.wait()

    def k_copy(d):
        return pltpu.make_async_remote_copy(
            src_ref=k_send.at[d],
            dst_ref=table_k.at[s_me],
            send_sem=k_ssem.at[d],
            recv_sem=k_rsem.at[s_me],
            device_id={"seq": d},
            device_id_type=MESH,
        )

    def v_copy(d):
        return pltpu.make_async_remote_copy(
            src_ref=v_send.at[d],
            dst_ref=table_v.at[s_me],
            send_sem=v_ssem.at[d],
            recv_sem=v_rsem.at[s_me],
            device_id={"seq": d},
            device_id_type=MESH,
        )

    def k_start(i, carry):
        d = lax.rem(s_me + n_seq - i, n_seq)
        asked = jnp.int32(0)
        for r in range(blocks):
            for c in range(K_SEL):
                entry = lists[c, d * blocks + r] - s_me * blocks
                asked = jnp.where((entry >= 0) & (entry < blocks), entry, asked)
        asked_s[d] = asked
        k_send[d] = k[asked]
        k_copy(d).start()
        return carry

    lax.fori_loop(1, n_seq, k_start, 0)

    def v_start(i, carry):
        d = lax.rem(s_me + n_seq - i, n_seq)
        v_send[d] = v[asked_s[d]]
        v_copy(d).start()
        return carry

    lax.fori_loop(1, n_seq, v_start, 0)

    for b in range(blocks):
        table_k[n_seq + b] = k[b]
        table_v[n_seq + b] = v[b]
        for c in range(K_SEL):
            entry = lists[c, s_me * blocks + b]
            near = entry - s_me * blocks
            own = (near >= 0) & (near < blocks)
            slot_s[b * K_SEL + c] = jnp.where(own, n_seq + near, lax.div(entry, jnp.int32(blocks)))
        ds_scr[b, K_SEL] = jnp.zeros((BLK, BLK), BF)
        for h in range(heads):
            p_scr[h, b, K_SEL] = jnp.zeros((BLK, BLK), BF)

    def fill_index(t, carry):
        for b in range(blocks):
            place = jnp.int32(K_SEL)
            for c in range(K_SEL):
                place = jnp.where(slot_s[b * K_SEL + c] == t, c, place)
            idx_s[t * blocks + b] = place
        return carry

    lax.fori_loop(0, n_seq + blocks, fill_index, 0)

    for load in loads[3:]:
        load.wait()

    def w_cols(shard):
        return w[:, pl.ds(pl.multiple_of(shard * width, width), width)]

    ga_acc[...] = dot_nt(og_all[z], w_cols(z))

    def og_round(step, carry):
        def one(c, inner):
            @pl.when(z - step >= 0)
            def _():
                og_copy(z - step, c, True, False).wait_recv()

                @pl.when(z < n_head - 1)
                def _():
                    og_copy(z - step, c, True, False).start()

            @pl.when(z + step < n_head)
            def _():
                og_copy(z + step, c, False, False).wait_recv()

                @pl.when(z > 0)
                def _():
                    og_copy(z + step, c, False, False).start()

            return inner

        lax.fori_loop(0, blocks, one, 0)

        @pl.when(z - step >= 0)
        def _():
            ga_acc[...] += dot_nt(og_all[z - step], w_cols(z - step))

        @pl.when(z + step < n_head)
        def _():
            ga_acc[...] += dot_nt(og_all[z + step], w_cols(z + step))

        return carry

    lax.fori_loop(1, n_head - 1, og_round, 0)

    def landed(buffer, table, ssem, rsem):
        def one(i, carry):
            src = lax.rem(s_me + i, n_seq)
            pltpu.make_async_remote_copy(
                src_ref=buffer.at[src],
                dst_ref=table.at[src],
                send_sem=ssem.at[src],
                recv_sem=rsem.at[src],
                device_id={"seq": src},
                device_id_type=MESH,
            ).wait_recv()
            return carry

        lax.fori_loop(1, n_seq, one, 0)

    def picked(table, b, h):
        cols = pl.ds(pl.multiple_of(h * HD, HD), HD)
        return jnp.concatenate(
            [table[slot_s[b * K_SEL + c], :, cols] for c in range(K_SEL)], axis=0
        )

    landed(k_send, table_k, k_ssem, k_rsem)

    def weigh(h, carry):
        cols = pl.ds(pl.multiple_of(h * HD, HD), HD)
        for b in range(blocks):
            rows = slice(b * BLK, (b + 1) * BLK)
            scores = dot_nt(picked(table_k, b, h), q[rows, cols]) * scale
            top = jnp.max(scores, axis=0, keepdims=True)
            weights = jnp.exp(scores - top)
            total = jnp.sum(weights, axis=0, keepdims=True)
            probs = (weights * (1.0 / total)).astype(BF)
            for c in range(K_SEL):
                p_scr[h, b, c] = probs[c * BLK:(c + 1) * BLK]
        return carry

    lax.fori_loop(0, heads, weigh, 0)

    def probs_of(h, b):
        return jnp.concatenate([p_scr[h, b, c] for c in range(K_SEL)], axis=0)

    landed(v_send, table_v, v_ssem, v_rsem)

    def attend(h, carry):
        cols = pl.ds(pl.multiple_of(h * HD, HD), HD)
        for b in range(blocks):
            rows = slice(b * BLK, (b + 1) * BLK)
            attn[rows, cols] = dot_tn(probs_of(h, b), picked(table_v, b, h)).astype(BF)
        return carry

    lax.fori_loop(0, heads, attend, 0)

    def part_copy(d, c, up):
        landing = from_below if up else from_above
        return pltpu.make_async_remote_copy(
            src_ref=part_send.at[d, chunk(c), :],
            dst_ref=landing.at[d, chunk(c), :],
            send_sem=pt_ssem.at[d, c],
            recv_sem=(below_sem if up else above_sem).at[d, c],
            device_id={"head": z + 1 if up else z - 1},
            device_id_type=MESH,
        )

    def project(i, carry):
        last = lax.div(z, n_head - 1)
        d = last * i + (1 - last) * (n_head - 1 - i)
        part_send[d] = dot_nn(attn[...], w_cols(d)).astype(BF)
        for c in range(blocks):
            @pl.when((z == 0) & (d > 0))
            def _():
                part_copy(d, c, True).start()

            @pl.when((z == n_head - 1) & (d < n_head - 1))
            def _():
                part_copy(d, c, False).start()

        return carry

    lax.fori_loop(0, n_head, project, 0)

    og_round(n_head - 1, 0)
    ga[...] = ga_acc[...].astype(BF)

    def ret_copy(h, d):
        return pltpu.make_async_remote_copy(
            src_ref=ret_send.at[h, d],
            dst_ref=ret_recv.at[h, s_me],
            send_sem=rt_ssem.at[h, d],
            recv_sem=rt_rsem.at[h, s_me],
            device_id={"seq": d},
            device_id_type=MESH,
        )

    def backward(h, carry):
        cols = pl.ds(pl.multiple_of(h * HD, HD), HD)
        for b in range(blocks):
            rows = slice(b * BLK, (b + 1) * BLK)
            probs = probs_of(h, b).astype(F32)
            grad_prob = dot_nt(picked(table_v, b, h), ga[rows, cols])
            delta = jnp.sum(probs * grad_prob, axis=0, keepdims=True)
            grad_score = (probs * (grad_prob - delta)).astype(BF)
            for c in range(K_SEL):
                ds_scr[b, c] = grad_score[c * BLK:(c + 1) * BLK]
            dq_o[rows, cols] = (dot_tn(grad_score, picked(table_k, b, h)) * scale).astype(BF)
        q_cols = q[:, cols]
        g_cols = ga[:, cols]

        def terms(t):
            places = [idx_s[t * blocks + b] for b in range(blocks)]
            ds_t = jnp.concatenate([ds_scr[b, places[b]] for b in range(blocks)], axis=1)
            p_t = jnp.concatenate([p_scr[h, b, places[b]] for b in range(blocks)], axis=1)
            return dot_nn(ds_t, q_cols) * scale, dot_nn(p_t, g_cols)

        for i in range(1, n_seq):
            d = lax.rem(s_me + n_seq - i, n_seq)
            key_part, value_part = terms(d)
            ret_send[h, d, :, :HD] = key_part.astype(BF)
            ret_send[h, d, :, HD:] = value_part.astype(BF)
            ret_copy(h, d).start()
        for b in range(blocks):
            rows = slice(b * BLK, (b + 1) * BLK)
            acc_k[rows, cols], acc_v[rows, cols] = terms(n_seq + b)
        return carry

    lax.fori_loop(0, heads, backward, 0)

    def hand_on(tick, carry):
        u = tick - z

        @pl.when((z > 0) & (u >= 0) & (u < blocks * (n_head - 1 - z)))
        def _():
            d = n_head - 1 - u // blocks
            c = lax.rem(u, blocks)
            part_copy(d, c, True).wait_recv()
            part_send[d, chunk(c), :] = (
                part_send[d, chunk(c), :].astype(F32) + from_below[d, chunk(c), :].astype(F32)
            ).astype(BF)
            part_copy(d, c, True).start()

        t = tick - (n_head - 1 - z)

        @pl.when((z < n_head - 1) & (t >= 0) & (t < blocks * z))
        def _():
            d = t // blocks
            c = lax.rem(t, blocks)
            part_copy(d, c, False).wait_recv()
            part_send[d, chunk(c), :] = (
                part_send[d, chunk(c), :].astype(F32) + from_above[d, chunk(c), :].astype(F32)
            ).astype(BF)
            part_copy(d, c, False).start()

        return carry

    lax.fori_loop(1, blocks * (n_head - 1) + n_head, hand_on, 0)

    def collect(h, carry):
        cols = pl.ds(pl.multiple_of(h * HD, HD), HD)

        def ret_wait(i, inner):
            src = lax.rem(s_me + i, n_seq)
            pltpu.make_async_remote_copy(
                src_ref=ret_send.at[h, src],
                dst_ref=ret_recv.at[h, src],
                send_sem=rt_ssem.at[h, src],
                recv_sem=rt_rsem.at[h, src],
                device_id={"seq": src},
                device_id_type=MESH,
            ).wait_recv()
            return inner

        lax.fori_loop(1, n_seq, ret_wait, 0)
        for b in range(blocks):
            rows = slice(b * BLK, (b + 1) * BLK)
            key_sum = acc_k[rows, cols]
            value_sum = acc_v[rows, cols]
            for i in range(1, n_seq):
                src = lax.rem(s_me + i, n_seq)
                flag = jnp.where(asked_s[src] == b, 1.0, 0.0)
                key_sum += flag * ret_recv[h, src, :, :HD].astype(F32)
                value_sum += flag * ret_recv[h, src, :, HD:].astype(F32)
            dk_o[rows, cols] = key_sum.astype(BF)
            dv_o[rows, cols] = value_sum.astype(BF)
        return carry

    lax.fori_loop(0, heads, collect, 0)

    for c in range(blocks):
        rows = slice(c * BLK, (c + 1) * BLK)
        ga_acc[rows, :] = part_send[z, rows, :].astype(F32)

        @pl.when(z > 0)
        def _():
            part_copy(z, c, True).wait_recv()
            ga_acc[rows, :] += from_below[z, rows, :].astype(F32)

        @pl.when(z < n_head - 1)
        def _():
            part_copy(z, c, False).wait_recv()
            ga_acc[rows, :] += from_above[z, rows, :].astype(F32)

        att_o[rows, :] = ga_acc[rows, :].astype(BF)

    def og_drain(c, carry):
        for step in range(n_head - 1):
            @pl.when((z - step >= 0) & (z < n_head - 1))
            def _():
                og_copy(z - step, c, True, False).wait_send()

            @pl.when((z + step < n_head) & (z > 0))
            def _():
                og_copy(z + step, c, False, False).wait_send()

        for d in range(n_head):
            @pl.when(z != d)
            def _():
                part_copy(d, c, True).wait_send()

        return carry

    lax.fori_loop(0, blocks, og_drain, 0)

    def seq_drain(i, carry):
        d = lax.rem(s_me + i, n_seq)
        k_copy(d).wait_send()
        v_copy(d).wait_send()

        def one(h, inner):
            ret_copy(h, d).wait_send()
            return inner

        return lax.fori_loop(0, heads, one, carry)

    lax.fori_loop(1, n_seq, seq_drain, 0)


def write_out(a0, a1, a2, a3, o0, o1, o2, o3, sems):
    copies = []
    for i, (src, dst) in enumerate(((a0, o0), (a1, o1), (a2, o2), (a3, o3))):
        for c in range(src.shape[0] // BLK):
            rows = pl.ds(c * BLK, BLK)
            copies.append(pltpu.make_async_copy(src.at[rows, :], dst.at[rows, :], sems.at[i, c]))
    for copy in copies:
        copy.start()
    for copy in copies:
        copy.wait()


def local(queries, key_states, value_states, block_lists, out_weight, out_grad):
    n_seq = lax.axis_size("seq")
    n_head = lax.axis_size("head")
    cells, width = queries.shape
    blocks = cells // BLK
    heads = width // HD
    slots = n_seq + blocks
    vmem = pl.BlockSpec(memory_space=pltpu.VMEM)
    hbm = pl.BlockSpec(memory_space=pl.ANY)
    main = pl.BlockSpec(memory_space=pltpu.HBM)
    sem = pltpu.SemaphoreType.DMA
    out = jax.ShapeDtypeStruct((cells, width), BF)
    held = pltpu.VMEM((cells, width), BF)
    results = pl.pallas_call(
        functools.partial(kernel, n_seq, n_head),
        out_shape=(held, held, held, held),
        in_specs=[
            main, main, main, main, main, main,
        ],
        out_specs=(vmem, vmem, vmem, vmem),
        scratch_shapes=[
            pltpu.VMEM((cells, width), BF),
            pltpu.VMEM((blocks, BLK, width), BF),
            pltpu.VMEM((blocks, BLK, width), BF),
            pltpu.VMEM((slots, BLK, width), BF),
            pltpu.VMEM((slots, BLK, width), BF),
            pltpu.VMEM((n_seq, BLK, width), BF),
            pltpu.VMEM((n_seq, BLK, width), BF),
            pltpu.VMEM(out_weight.shape, BF),
            pltpu.VMEM((n_head, cells, width), BF),
            pltpu.VMEM((heads, blocks, K_SEL + 1, BLK, BLK), BF),
            pltpu.VMEM((blocks, K_SEL + 1, BLK, BLK), BF),
            pltpu.VMEM((cells, width), BF),
            pltpu.VMEM((n_head, cells, width), BF),
            pltpu.VMEM((n_head, cells, width), BF),
            pltpu.VMEM((n_head, cells, width), BF),
            pltpu.VMEM((cells, width), F32),
            pltpu.VMEM((cells, width), BF),
            pltpu.VMEM((heads, n_seq, BLK, 2 * HD), BF),
            pltpu.VMEM((heads, n_seq, BLK, 2 * HD), BF),
            pltpu.VMEM((cells, width), F32),
            pltpu.VMEM((cells, width), F32),
            pltpu.SMEM(block_lists.shape[::-1], jnp.int32),
            pltpu.SMEM((blocks * K_SEL,), jnp.int32),
            pltpu.SMEM((n_seq,), jnp.int32),
            pltpu.SMEM((slots * blocks,), jnp.int32),
            sem((6,)), sem((n_head, blocks)), sem((n_head, blocks)), sem((n_head, blocks)),
            sem((n_seq,)), sem((n_seq,)), sem((n_seq,)), sem((n_seq,)),
            sem((n_head, blocks)), sem((n_head, blocks)), sem((n_head, blocks)),
            sem((heads, n_seq)), sem((heads, n_seq)),
        ],
        compiler_params=pltpu.CompilerParams(
            collective_id=0, has_side_effects=True, vmem_limit_bytes=56 * 1024 * 1024
        ),
        cost_estimate=pl.CostEstimate(
            flops=8 * 10**9, bytes_accessed=20 * 10**6, transcendentals=10**6
        ),
    )(
        block_lists.T,
        queries,
        key_states.reshape(blocks, BLK, width),
        value_states.reshape(blocks, BLK, width),
        out_grad,
        out_weight,
    )
    return pl.pallas_call(
        write_out,
        out_shape=(out, out, out, out),
        in_specs=[vmem] * 4,
        out_specs=(hbm,) * 4,
        scratch_shapes=[sem((4, blocks))],
    )(*results)


def solution(mesh):
    in_specs = (
        P("seq", "head"),
        P("seq", "head"),
        P("seq", "head"),
        P(),
        P("head", None),
        P("seq", "head"),
    )
    out_specs = (P("seq", "head"), P("seq", "head"), P("seq", "head"), P("seq", "head"))
    return jax.shard_map(local, mesh=mesh, in_specs=in_specs, out_specs=out_specs, check_vma=False)
```

```python
import functools
import math

import jax
import jax.numpy as jnp
from jax import lax
from jax.experimental import pallas as pl
from jax.experimental.pallas import tpu as pltpu
from jax.sharding import PartitionSpec as P

HD = 128
BLK = 128
K_SEL = 4
MESH = pl.DeviceIdType.MESH
BF = jnp.bfloat16
F32 = jnp.float32


def dot_nn(a, b):
    return lax.dot_general(a, b, (((1,), (0,)), ((), ())), preferred_element_type=F32)


def dot_nt(a, b):
    return lax.dot_general(a, b, (((1,), (1,)), ((), ())), preferred_element_type=F32)


def dot_tn(a, b):
    return lax.dot_general(a, b, (((0,), (0,)), ((), ())), preferred_element_type=F32)


def kernel(
    n_seq, n_head, lists_hbm, q_hbm, k_hbm, v_hbm, og, w_hbm,
    att_o, dq_o, dk_o, dv_o,
    q, k, v, table_k, table_v, k_send, v_send, w, og_all, p_scr, ds_scr, attn, part_send, from_below, from_above,
    ga_acc, ga, ret_send, ret_recv, acc_k, acc_v, lists, slot_s, asked_s, idx_s,
    load_sem, og_up, og_down, og_recv, k_ssem, k_rsem, v_ssem, v_rsem,
    pt_ssem, below_sem, above_sem, rt_ssem, rt_rsem,
):
    cells, width = q.shape
    blocks = cells // BLK
    heads = width // HD
    scale = 1.0 / math.sqrt(HD)
    s_me = lax.axis_index("seq")
    z = lax.axis_index("head")

    barrier = pltpu.get_barrier_semaphore()
    for o in range(1, n_head):
        pl.semaphore_signal(
            barrier, inc=1, device_id={"head": lax.rem(z + o, n_head)}, device_id_type=MESH
        )
    for o in range(1, n_seq):
        pl.semaphore_signal(
            barrier, inc=1, device_id={"seq": lax.rem(s_me + o, n_seq)}, device_id_type=MESH
        )
    loads = [
        pltpu.make_async_copy(src, dst, load_sem.at[i])
        for i, (src, dst) in enumerate(
            ((lists_hbm, lists), (k_hbm, k), (v_hbm, v), (og, og_all.at[z]), (q_hbm, q), (w_hbm, w))
        )
    ]
    for load in loads:
        load.start()
    for load in loads[:3]:
        load.wait()

    def stage(i, carry):
        d = lax.rem(s_me + n_seq - i, n_seq)
        asked = jnp.int32(0)
        for r in range(blocks):
            for c in range(K_SEL):
                entry = lists[c, d * blocks + r] - s_me * blocks
                asked = jnp.where((entry >= 0) & (entry < blocks), entry, asked)
        asked_s[d] = asked
        k_send[d] = k[asked]
        v_send[d] = v[asked]
        return carry

    lax.fori_loop(1, n_seq, stage, 0)
    pl.semaphore_wait(barrier, n_head - 1 + n_seq - 1)

    def chunk(c):
        return pl.ds(pl.multiple_of(c * BLK, BLK), BLK)

    def og_copy(shard, c, up, own):
        src = og.at[chunk(c), :] if own else og_all.at[shard, chunk(c), :]
        return pltpu.make_async_remote_copy(
            src_ref=src,
            dst_ref=og_all.at[shard, chunk(c), :],
            send_sem=(og_up if up else og_down).at[shard, c],
            recv_sem=og_recv.at[shard, c],
            device_id={"head": z + 1 if up else z - 1},
            device_id_type=MESH,
        )

    for c in range(blocks):
        @pl.when(z < n_head - 1)
        def _():
            og_copy(z, c, True, True).start()

        @pl.when(z > 0)
        def _():
            og_copy(z, c, False, True).start()

    def k_copy(d):
        return pltpu.make_async_remote_copy(
            src_ref=k_send.at[d],
            dst_ref=table_k.at[s_me],
            send_sem=k_ssem.at[d],
            recv_sem=k_rsem.at[s_me],
            device_id={"seq": d},
            device_id_type=MESH,
        )

    def v_copy(d):
        return pltpu.make_async_remote_copy(
            src_ref=v_send.at[d],
            dst_ref=table_v.at[s_me],
            send_sem=v_ssem.at[d],
            recv_sem=v_rsem.at[s_me],
            device_id={"seq": d},
            device_id_type=MESH,
        )

    def send(copy):
        def one(i, carry):
            copy(lax.rem(s_me + n_seq - i, n_seq)).start()
            return carry

        lax.fori_loop(1, n_seq, one, 0)

    send(k_copy)
    send(v_copy)

    for b in range(blocks):
        table_k[n_seq + b] = k[b]
        table_v[n_seq + b] = v[b]
        for c in range(K_SEL):
            entry = lists[c, s_me * blocks + b]
            near = entry - s_me * blocks
            own = (near >= 0) & (near < blocks)
            slot_s[b * K_SEL + c] = jnp.where(own, n_seq + near, lax.div(entry, jnp.int32(blocks)))
        ds_scr[b, K_SEL] = jnp.zeros((BLK, BLK), BF)
        for h in range(heads):
            p_scr[h, b, K_SEL] = jnp.zeros((BLK, BLK), BF)

    def fill_index(t, carry):
        for b in range(blocks):
            place = jnp.int32(K_SEL)
            for c in range(K_SEL):
                place = jnp.where(slot_s[b * K_SEL + c] == t, c, place)
            idx_s[t * blocks + b] = place
        return carry

    lax.fori_loop(0, n_seq + blocks, fill_index, 0)

    for load in loads[3:]:
        load.wait()

    def w_cols(shard):
        return w[:, pl.ds(pl.multiple_of(shard * width, width), width)]

    ga_acc[...] = dot_nt(og_all[z], w_cols(z))

    def og_round(step, carry):
        def one(c, inner):
            @pl.when(z - step >= 0)
            def _():
                og_copy(z - step, c, True, False).wait_recv()

                @pl.when(z < n_head - 1)
                def _():
                    og_copy(z - step, c, True, False).start()

            @pl.when(z + step < n_head)
            def _():
                og_copy(z + step, c, False, False).wait_recv()

                @pl.when(z > 0)
                def _():
                    og_copy(z + step, c, False, False).start()

            return inner

        lax.fori_loop(0, blocks, one, 0)

        @pl.when(z - step >= 0)
        def _():
            ga_acc[...] += dot_nt(og_all[z - step], w_cols(z - step))

        @pl.when(z + step < n_head)
        def _():
            ga_acc[...] += dot_nt(og_all[z + step], w_cols(z + step))

        return carry

    lax.fori_loop(1, n_head - 1, og_round, 0)

    def landed(buffer, table, ssem, rsem):
        def one(i, carry):
            src = lax.rem(s_me + i, n_seq)
            pltpu.make_async_remote_copy(
                src_ref=buffer.at[src],
                dst_ref=table.at[src],
                send_sem=ssem.at[src],
                recv_sem=rsem.at[src],
                device_id={"seq": src},
                device_id_type=MESH,
            ).wait_recv()
            return carry

        lax.fori_loop(1, n_seq, one, 0)

    def picked(table, b, h):
        cols = pl.ds(pl.multiple_of(h * HD, HD), HD)
        return jnp.concatenate(
            [table[slot_s[b * K_SEL + c], :, cols] for c in range(K_SEL)], axis=0
        )

    landed(k_send, table_k, k_ssem, k_rsem)

    def weigh(h, carry):
        cols = pl.ds(pl.multiple_of(h * HD, HD), HD)
        for b in range(blocks):
            rows = slice(b * BLK, (b + 1) * BLK)
            scores = dot_nt(picked(table_k, b, h), q[rows, cols]) * scale
            top = jnp.max(scores, axis=0, keepdims=True)
            weights = jnp.exp(scores - top)
            total = jnp.sum(weights, axis=0, keepdims=True)
            probs = (weights * (1.0 / total)).astype(BF)
            for c in range(K_SEL):
                p_scr[h, b, c] = probs[c * BLK:(c + 1) * BLK]
        return carry

    lax.fori_loop(0, heads, weigh, 0)

    def probs_of(h, b):
        return jnp.concatenate([p_scr[h, b, c] for c in range(K_SEL)], axis=0)

    landed(v_send, table_v, v_ssem, v_rsem)

    def attend(h, carry):
        cols = pl.ds(pl.multiple_of(h * HD, HD), HD)
        for b in range(blocks):
            rows = slice(b * BLK, (b + 1) * BLK)
            attn[rows, cols] = dot_tn(probs_of(h, b), picked(table_v, b, h)).astype(BF)
        return carry

    lax.fori_loop(0, heads, attend, 0)

    def part_copy(d, c, up):
        landing = from_below if up else from_above
        return pltpu.make_async_remote_copy(
            src_ref=part_send.at[d, chunk(c), :],
            dst_ref=landing.at[d, chunk(c), :],
            send_sem=pt_ssem.at[d, c],
            recv_sem=(below_sem if up else above_sem).at[d, c],
            device_id={"head": z + 1 if up else z - 1},
            device_id_type=MESH,
        )

    def project(i, carry):
        last = lax.div(z, n_head - 1)
        d = last * i + (1 - last) * (n_head - 1 - i)
        part_send[d] = dot_nn(attn[...], w_cols(d)).astype(BF)
        for c in range(blocks):
            @pl.when((z == 0) & (d > 0))
            def _():
                part_copy(d, c, True).start()

            @pl.when((z == n_head - 1) & (d < n_head - 1))
            def _():
                part_copy(d, c, False).start()

        return carry

    lax.fori_loop(0, n_head, project, 0)

    og_round(n_head - 1, 0)
    ga[...] = ga_acc[...].astype(BF)

    def ret_copy(h, d):
        return pltpu.make_async_remote_copy(
            src_ref=ret_send.at[h, d],
            dst_ref=ret_recv.at[h, s_me],
            send_sem=rt_ssem.at[h, d],
            recv_sem=rt_rsem.at[h, s_me],
            device_id={"seq": d},
            device_id_type=MESH,
        )

    def backward(h, carry):
        cols = pl.ds(pl.multiple_of(h * HD, HD), HD)
        for b in range(blocks):
            rows = slice(b * BLK, (b + 1) * BLK)
            probs = probs_of(h, b).astype(F32)
            grad_prob = dot_nt(picked(table_v, b, h), ga[rows, cols])
            delta = jnp.sum(probs * grad_prob, axis=0, keepdims=True)
            grad_score = (probs * (grad_prob - delta)).astype(BF)
            for c in range(K_SEL):
                ds_scr[b, c] = grad_score[c * BLK:(c + 1) * BLK]
            dq_o[rows, cols] = (dot_tn(grad_score, picked(table_k, b, h)) * scale).astype(BF)
        q_cols = q[:, cols]
        g_cols = ga[:, cols]

        def terms(t):
            places = [idx_s[t * blocks + b] for b in range(blocks)]
            ds_t = jnp.concatenate([ds_scr[b, places[b]] for b in range(blocks)], axis=1)
            p_t = jnp.concatenate([p_scr[h, b, places[b]] for b in range(blocks)], axis=1)
            return dot_nn(ds_t, q_cols) * scale, dot_nn(p_t, g_cols)

        for i in range(1, n_seq):
            d = lax.rem(s_me + n_seq - i, n_seq)
            key_part, value_part = terms(d)
            ret_send[h, d, :, :HD] = key_part.astype(BF)
            ret_send[h, d, :, HD:] = value_part.astype(BF)
            ret_copy(h, d).start()
        for b in range(blocks):
            rows = slice(b * BLK, (b + 1) * BLK)
            acc_k[rows, cols], acc_v[rows, cols] = terms(n_seq + b)
        return carry

    lax.fori_loop(0, heads, backward, 0)

    def hand_on(tick, carry):
        u = tick - z

        @pl.when((z > 0) & (u >= 0) & (u < blocks * (n_head - 1 - z)))
        def _():
            d = n_head - 1 - u // blocks
            c = lax.rem(u, blocks)
            part_copy(d, c, True).wait_recv()
            part_send[d, chunk(c), :] = (
                part_send[d, chunk(c), :].astype(F32) + from_below[d, chunk(c), :].astype(F32)
            ).astype(BF)
            part_copy(d, c, True).start()

        t = tick - (n_head - 1 - z)

        @pl.when((z < n_head - 1) & (t >= 0) & (t < blocks * z))
        def _():
            d = t // blocks
            c = lax.rem(t, blocks)
            part_copy(d, c, False).wait_recv()
            part_send[d, chunk(c), :] = (
                part_send[d, chunk(c), :].astype(F32) + from_above[d, chunk(c), :].astype(F32)
            ).astype(BF)
            part_copy(d, c, False).start()

        return carry

    lax.fori_loop(1, blocks * (n_head - 1) + n_head, hand_on, 0)

    def collect(h, carry):
        cols = pl.ds(pl.multiple_of(h * HD, HD), HD)

        def ret_wait(i, inner):
            src = lax.rem(s_me + i, n_seq)
            pltpu.make_async_remote_copy(
                src_ref=ret_send.at[h, src],
                dst_ref=ret_recv.at[h, src],
                send_sem=rt_ssem.at[h, src],
                recv_sem=rt_rsem.at[h, src],
                device_id={"seq": src},
                device_id_type=MESH,
            ).wait_recv()
            return inner

        lax.fori_loop(1, n_seq, ret_wait, 0)
        for b in range(blocks):
            rows = slice(b * BLK, (b + 1) * BLK)
            key_sum = acc_k[rows, cols]
            value_sum = acc_v[rows, cols]
            for i in range(1, n_seq):
                src = lax.rem(s_me + i, n_seq)
                flag = jnp.where(asked_s[src] == b, 1.0, 0.0)
                key_sum += flag * ret_recv[h, src, :, :HD].astype(F32)
                value_sum += flag * ret_recv[h, src, :, HD:].astype(F32)
            dk_o[rows, cols] = key_sum.astype(BF)
            dv_o[rows, cols] = value_sum.astype(BF)
        return carry

    lax.fori_loop(0, heads, collect, 0)

    for c in range(blocks):
        rows = slice(c * BLK, (c + 1) * BLK)
        ga_acc[rows, :] = part_send[z, rows, :].astype(F32)

        @pl.when(z > 0)
        def _():
            part_copy(z, c, True).wait_recv()
            ga_acc[rows, :] += from_below[z, rows, :].astype(F32)

        @pl.when(z < n_head - 1)
        def _():
            part_copy(z, c, False).wait_recv()
            ga_acc[rows, :] += from_above[z, rows, :].astype(F32)

        att_o[rows, :] = ga_acc[rows, :].astype(BF)

    def og_drain(c, carry):
        for step in range(n_head - 1):
            @pl.when((z - step >= 0) & (z < n_head - 1))
            def _():
                og_copy(z - step, c, True, False).wait_send()

            @pl.when((z + step < n_head) & (z > 0))
            def _():
                og_copy(z + step, c, False, False).wait_send()

        for d in range(n_head):
            @pl.when(z != d)
            def _():
                part_copy(d, c, True).wait_send()

        return carry

    lax.fori_loop(0, blocks, og_drain, 0)

    def seq_drain(i, carry):
        d = lax.rem(s_me + i, n_seq)
        k_copy(d).wait_send()
        v_copy(d).wait_send()

        def one(h, inner):
            ret_copy(h, d).wait_send()
            return inner

        return lax.fori_loop(0, heads, one, carry)

    lax.fori_loop(1, n_seq, seq_drain, 0)


def write_out(a0, a1, a2, a3, o0, o1, o2, o3, sems):
    copies = []
    for i, (src, dst) in enumerate(((a0, o0), (a1, o1), (a2, o2), (a3, o3))):
        for c in range(src.shape[0] // BLK):
            rows = pl.ds(c * BLK, BLK)
            copies.append(pltpu.make_async_copy(src.at[rows, :], dst.at[rows, :], sems.at[i, c]))
    for copy in copies:
        copy.start()
    for copy in copies:
        copy.wait()


def local(queries, key_states, value_states, block_lists, out_weight, out_grad):
    n_seq = lax.axis_size("seq")
    n_head = lax.axis_size("head")
    cells, width = queries.shape
    blocks = cells // BLK
    heads = width // HD
    slots = n_seq + blocks
    vmem = pl.BlockSpec(memory_space=pltpu.VMEM)
    main = pl.BlockSpec(memory_space=pltpu.HBM)
    sem = pltpu.SemaphoreType.DMA
    out = jax.ShapeDtypeStruct((cells, width), BF)
    held = pltpu.VMEM((cells, width), BF)
    results = pl.pallas_call(
        functools.partial(kernel, n_seq, n_head),
        out_shape=(held, held, held, held),
        in_specs=[
            main, main, main, main, main, main,
        ],
        out_specs=(vmem, vmem, vmem, vmem),
        scratch_shapes=[
            pltpu.VMEM((cells, width), BF),
            pltpu.VMEM((blocks, BLK, width), BF),
            pltpu.VMEM((blocks, BLK, width), BF),
            pltpu.VMEM((slots, BLK, width), BF),
            pltpu.VMEM((slots, BLK, width), BF),
            pltpu.VMEM((n_seq, BLK, width), BF),
            pltpu.VMEM((n_seq, BLK, width), BF),
            pltpu.VMEM(out_weight.shape, BF),
            pltpu.VMEM((n_head, cells, width), BF),
            pltpu.VMEM((heads, blocks, K_SEL + 1, BLK, BLK), BF),
            pltpu.VMEM((blocks, K_SEL + 1, BLK, BLK), BF),
            pltpu.VMEM((cells, width), BF),
            pltpu.VMEM((n_head, cells, width), BF),
            pltpu.VMEM((n_head, cells, width), BF),
            pltpu.VMEM((n_head, cells, width), BF),
            pltpu.VMEM((cells, width), F32),
            pltpu.VMEM((cells, width), BF),
            pltpu.VMEM((heads, n_seq, BLK, 2 * HD), BF),
            pltpu.VMEM((heads, n_seq, BLK, 2 * HD), BF),
            pltpu.VMEM((cells, width), F32),
            pltpu.VMEM((cells, width), F32),
            pltpu.SMEM(block_lists.shape[::-1], jnp.int32),
            pltpu.SMEM((blocks * K_SEL,), jnp.int32),
            pltpu.SMEM((n_seq,), jnp.int32),
            pltpu.SMEM((slots * blocks,), jnp.int32),
            sem((6,)), sem((n_head, blocks)), sem((n_head, blocks)), sem((n_head, blocks)),
            sem((n_seq,)), sem((n_seq,)), sem((n_seq,)), sem((n_seq,)),
            sem((n_head, blocks)), sem((n_head, blocks)), sem((n_head, blocks)),
            sem((heads, n_seq)), sem((heads, n_seq)),
        ],
        compiler_params=pltpu.CompilerParams(
            collective_id=0, has_side_effects=True, vmem_limit_bytes=56 * 1024 * 1024
        ),
        cost_estimate=pl.CostEstimate(
            flops=8 * 10**9, bytes_accessed=20 * 10**6, transcendentals=10**6
        ),
    )(
        block_lists.T,
        queries,
        key_states.reshape(blocks, BLK, width),
        value_states.reshape(blocks, BLK, width),
        out_grad,
        out_weight,
    )
    return pl.pallas_call(
        write_out,
        out_shape=(out, out, out, out),
        in_specs=[vmem] * 4,
        out_specs=(main,) * 4,
        scratch_shapes=[sem((4, blocks))],
    )(*results)


def solution(mesh):
    in_specs = (
        P("seq", "head"),
        P("seq", "head"),
        P("seq", "head"),
        P(),
        P("head", None),
        P("seq", "head"),
    )
    out_specs = (P("seq", "head"), P("seq", "head"), P("seq", "head"), P("seq", "head"))
    return jax.shard_map(local, mesh=mesh, in_specs=in_specs, out_specs=out_specs, check_vma=False)
```

```python
import functools
import math

import jax
import jax.numpy as jnp
from jax import lax
from jax.experimental import pallas as pl
from jax.experimental.pallas import tpu as pltpu
from jax.sharding import PartitionSpec as P

HD = 128
BLK = 128
K_SEL = 4
MESH = pl.DeviceIdType.MESH
BF = jnp.bfloat16
F32 = jnp.float32


def dot_nn(a, b):
    return lax.dot_general(a, b, (((1,), (0,)), ((), ())), preferred_element_type=F32)


def dot_nt(a, b):
    return lax.dot_general(a, b, (((1,), (1,)), ((), ())), preferred_element_type=F32)


def dot_tn(a, b):
    return lax.dot_general(a, b, (((0,), (0,)), ((), ())), preferred_element_type=F32)


def kernel(
    n_seq, n_head, lists_hbm, q_hbm, k_hbm, v_hbm, og, w_hbm,
    att_o, dq_o, dk_o, dv_o,
    q, k, v, table_k, table_v, k_send, v_send, w, og_all, p_scr, ds_scr, attn, part_send, from_below, from_above,
    ga_acc, ga, ret_send, ret_recv, acc_k, acc_v, lists, slot_s, asked_s, idx_s,
    load_sem, og_up, og_down, og_recv, k_ssem, k_rsem, v_ssem, v_rsem,
    pt_ssem, below_sem, above_sem, rt_ssem, rt_rsem,
):
    cells, width = q.shape
    blocks = cells // BLK
    heads = width // HD
    scale = 1.0 / math.sqrt(HD)
    s_me = lax.axis_index("seq")
    z = lax.axis_index("head")

    barrier = pltpu.get_barrier_semaphore()
    for o in range(1, n_head):
        pl.semaphore_signal(
            barrier, inc=1, device_id={"head": lax.rem(z + o, n_head)}, device_id_type=MESH
        )
    for o in range(1, n_seq):
        pl.semaphore_signal(
            barrier, inc=1, device_id={"seq": lax.rem(s_me + o, n_seq)}, device_id_type=MESH
        )
    loads = [
        pltpu.make_async_copy(src, dst, load_sem.at[i])
        for i, (src, dst) in enumerate(
            ((lists_hbm, lists), (k_hbm, k), (v_hbm, v), (og, og_all.at[z]), (q_hbm, q), (w_hbm, w))
        )
    ]
    for load in loads:
        load.start()
    for load in loads[:3]:
        load.wait()

    def stage(i, carry):
        d = lax.rem(s_me + n_seq - i, n_seq)
        asked = jnp.int32(0)
        for r in range(blocks):
            for c in range(K_SEL):
                entry = lists[c, d * blocks + r] - s_me * blocks
                asked = jnp.where((entry >= 0) & (entry < blocks), entry, asked)
        asked_s[d] = asked
        k_send[d] = k[asked]
        v_send[d] = v[asked]
        return carry

    lax.fori_loop(1, n_seq, stage, 0)
    pl.semaphore_wait(barrier, n_head - 1 + n_seq - 1)

    def chunk(c):
        return pl.ds(pl.multiple_of(c * BLK, BLK), BLK)

    def og_copy(shard, c, up, own):
        src = og.at[chunk(c), :] if own else og_all.at[shard, chunk(c), :]
        return pltpu.make_async_remote_copy(
            src_ref=src,
            dst_ref=og_all.at[shard, chunk(c), :],
            send_sem=(og_up if up else og_down).at[shard, c],
            recv_sem=og_recv.at[shard, c],
            device_id={"head": z + 1 if up else z - 1},
            device_id_type=MESH,
        )

    for c in range(blocks):
        @pl.when(z < n_head - 1)
        def _():
            og_copy(z, c, True, True).start()

        @pl.when(z > 0)
        def _():
            og_copy(z, c, False, True).start()

    def k_copy(d):
        return pltpu.make_async_remote_copy(
            src_ref=k_send.at[d],
            dst_ref=table_k.at[s_me],
            send_sem=k_ssem.at[d],
            recv_sem=k_rsem.at[s_me],
            device_id={"seq": d},
            device_id_type=MESH,
        )

    def v_copy(d):
        return pltpu.make_async_remote_copy(
            src_ref=v_send.at[d],
            dst_ref=table_v.at[s_me],
            send_sem=v_ssem.at[d],
            recv_sem=v_rsem.at[s_me],
            device_id={"seq": d},
            device_id_type=MESH,
        )

    def send(copy):
        def one(i, carry):
            copy(lax.rem(s_me + n_seq - i, n_seq)).start()
            return carry

        lax.fori_loop(1, n_seq, one, 0)

    send(k_copy)
    send(v_copy)

    for b in range(blocks):
        table_k[n_seq + b] = k[b]
        table_v[n_seq + b] = v[b]
        for c in range(K_SEL):
            entry = lists[c, s_me * blocks + b]
            near = entry - s_me * blocks
            own = (near >= 0) & (near < blocks)
            slot_s[b * K_SEL + c] = jnp.where(own, n_seq + near, lax.div(entry, jnp.int32(blocks)))
        ds_scr[b, K_SEL] = jnp.zeros((BLK, BLK), BF)
        for h in range(heads):
            p_scr[h, b, K_SEL] = jnp.zeros((BLK, BLK), BF)

    def fill_index(t, carry):
        for b in range(blocks):
            place = jnp.int32(K_SEL)
            for c in range(K_SEL):
                place = jnp.where(slot_s[b * K_SEL + c] == t, c, place)
            idx_s[t * blocks + b] = place
        return carry

    lax.fori_loop(0, n_seq + blocks, fill_index, 0)

    for load in loads[3:]:
        load.wait()

    def w_cols(shard):
        return w[:, pl.ds(pl.multiple_of(shard * width, width), width)]

    ga_acc[...] = dot_nt(og_all[z], w_cols(z))

    def og_round(step, carry):
        def one(c, inner):
            @pl.when(z - step >= 0)
            def _():
                og_copy(z - step, c, True, False).wait_recv()

                @pl.when(z < n_head - 1)
                def _():
                    og_copy(z - step, c, True, False).start()

            @pl.when(z + step < n_head)
            def _():
                og_copy(z + step, c, False, False).wait_recv()

                @pl.when(z > 0)
                def _():
                    og_copy(z + step, c, False, False).start()

            return inner

        lax.fori_loop(0, blocks, one, 0)

        @pl.when(z - step >= 0)
        def _():
            ga_acc[...] += dot_nt(og_all[z - step], w_cols(z - step))

        @pl.when(z + step < n_head)
        def _():
            ga_acc[...] += dot_nt(og_all[z + step], w_cols(z + step))

        return carry

    lax.fori_loop(1, n_head - 1, og_round, 0)

    def landed(buffer, table, ssem, rsem):
        def one(i, carry):
            src = lax.rem(s_me + i, n_seq)
            pltpu.make_async_remote_copy(
                src_ref=buffer.at[src],
                dst_ref=table.at[src],
                send_sem=ssem.at[src],
                recv_sem=rsem.at[src],
                device_id={"seq": src},
                device_id_type=MESH,
            ).wait_recv()
            return carry

        lax.fori_loop(1, n_seq, one, 0)

    def picked(table, b, h):
        cols = pl.ds(pl.multiple_of(h * HD, HD), HD)
        return jnp.concatenate(
            [table[slot_s[b * K_SEL + c], :, cols] for c in range(K_SEL)], axis=0
        )

    landed(k_send, table_k, k_ssem, k_rsem)

    def weigh(h, carry):
        cols = pl.ds(pl.multiple_of(h * HD, HD), HD)
        for b in range(blocks):
            rows = slice(b * BLK, (b + 1) * BLK)
            scores = dot_nt(picked(table_k, b, h), q[rows, cols]) * scale
            top = jnp.max(scores, axis=0, keepdims=True)
            weights = jnp.exp(scores - top)
            total = jnp.sum(weights, axis=0, keepdims=True)
            probs = (weights * (1.0 / total)).astype(BF)
            for c in range(K_SEL):
                p_scr[h, b, c] = probs[c * BLK:(c + 1) * BLK]
        return carry

    lax.fori_loop(0, heads, weigh, 0)

    def probs_of(h, b):
        return jnp.concatenate([p_scr[h, b, c] for c in range(K_SEL)], axis=0)

    landed(v_send, table_v, v_ssem, v_rsem)

    def attend(h, carry):
        cols = pl.ds(pl.multiple_of(h * HD, HD), HD)
        for b in range(blocks):
            rows = slice(b * BLK, (b + 1) * BLK)
            attn[rows, cols] = dot_tn(probs_of(h, b), picked(table_v, b, h)).astype(BF)
        return carry

    lax.fori_loop(0, heads, attend, 0)

    def part_copy(d, c, up):
        landing = from_below if up else from_above
        return pltpu.make_async_remote_copy(
            src_ref=part_send.at[d, chunk(c), :],
            dst_ref=landing.at[d, chunk(c), :],
            send_sem=pt_ssem.at[d, c],
            recv_sem=(below_sem if up else above_sem).at[d, c],
            device_id={"head": z + 1 if up else z - 1},
            device_id_type=MESH,
        )

    def project(i, carry):
        last = lax.div(z, n_head - 1)
        d = last * i + (1 - last) * (n_head - 1 - i)
        part_send[d] = dot_nn(attn[...], w_cols(d)).astype(BF)
        for c in range(blocks):
            @pl.when((z == 0) & (d > 0))
            def _():
                part_copy(d, c, True).start()

            @pl.when((z == n_head - 1) & (d < n_head - 1))
            def _():
                part_copy(d, c, False).start()

        return carry

    lax.fori_loop(0, n_head, project, 0)

    og_round(n_head - 1, 0)
    ga[...] = ga_acc[...].astype(BF)

    def ret_copy(h, d):
        return pltpu.make_async_remote_copy(
            src_ref=ret_send.at[h, d],
            dst_ref=ret_recv.at[h, s_me],
            send_sem=rt_ssem.at[h, d],
            recv_sem=rt_rsem.at[h, s_me],
            device_id={"seq": d},
            device_id_type=MESH,
        )

    def backward(h, carry):
        cols = pl.ds(pl.multiple_of(h * HD, HD), HD)
        for b in range(blocks):
            rows = slice(b * BLK, (b + 1) * BLK)
            probs = probs_of(h, b).astype(F32)
            grad_prob = dot_nt(picked(table_v, b, h), ga[rows, cols])
            delta = jnp.sum(probs * grad_prob, axis=0, keepdims=True)
            grad_score = (probs * (grad_prob - delta)).astype(BF)
            for c in range(K_SEL):
                ds_scr[b, c] = grad_score[c * BLK:(c + 1) * BLK]
            dq_o[rows, cols] = (dot_tn(grad_score, picked(table_k, b, h)) * scale).astype(BF)
        q_cols = q[:, cols]
        g_cols = ga[:, cols]

        def terms(t):
            places = [idx_s[t * blocks + b] for b in range(blocks)]
            ds_t = jnp.concatenate([ds_scr[b, places[b]] for b in range(blocks)], axis=1)
            p_t = jnp.concatenate([p_scr[h, b, places[b]] for b in range(blocks)], axis=1)
            return dot_nn(ds_t, q_cols) * scale, dot_nn(p_t, g_cols)

        for i in range(1, n_seq):
            d = lax.rem(s_me + n_seq - i, n_seq)
            key_part, value_part = terms(d)
            ret_send[h, d, :, :HD] = key_part.astype(BF)
            ret_send[h, d, :, HD:] = value_part.astype(BF)
            ret_copy(h, d).start()
        for b in range(blocks):
            rows = slice(b * BLK, (b + 1) * BLK)
            acc_k[rows, cols], acc_v[rows, cols] = terms(n_seq + b)
        return carry

    lax.fori_loop(0, heads, backward, 0)

    def hand_on(tick, carry):
        u = tick - z

        @pl.when((z > 0) & (u >= 0) & (u < blocks * (n_head - 1 - z)))
        def _():
            d = n_head - 1 - u // blocks
            c = lax.rem(u, blocks)
            part_copy(d, c, True).wait_recv()
            part_send[d, chunk(c), :] = (
                part_send[d, chunk(c), :].astype(F32) + from_below[d, chunk(c), :].astype(F32)
            ).astype(BF)
            part_copy(d, c, True).start()

        t = tick - (n_head - 1 - z)

        @pl.when((z < n_head - 1) & (t >= 0) & (t < blocks * z))
        def _():
            d = t // blocks
            c = lax.rem(t, blocks)
            part_copy(d, c, False).wait_recv()
            part_send[d, chunk(c), :] = (
                part_send[d, chunk(c), :].astype(F32) + from_above[d, chunk(c), :].astype(F32)
            ).astype(BF)
            part_copy(d, c, False).start()

        return carry

    lax.fori_loop(1, blocks * (n_head - 1) + n_head, hand_on, 0)

    def collect(h, carry):
        cols = pl.ds(pl.multiple_of(h * HD, HD), HD)

        def ret_wait(i, inner):
            src = lax.rem(s_me + i, n_seq)
            pltpu.make_async_remote_copy(
                src_ref=ret_send.at[h, src],
                dst_ref=ret_recv.at[h, src],
                send_sem=rt_ssem.at[h, src],
                recv_sem=rt_rsem.at[h, src],
                device_id={"seq": src},
                device_id_type=MESH,
            ).wait_recv()
            return inner

        lax.fori_loop(1, n_seq, ret_wait, 0)
        for b in range(blocks):
            rows = slice(b * BLK, (b + 1) * BLK)
            key_sum = acc_k[rows, cols]
            value_sum = acc_v[rows, cols]
            for i in range(1, n_seq):
                src = lax.rem(s_me + i, n_seq)
                flag = jnp.where(asked_s[src] == b, 1.0, 0.0)
                key_sum += flag * ret_recv[h, src, :, :HD].astype(F32)
                value_sum += flag * ret_recv[h, src, :, HD:].astype(F32)
            dk_o[rows, cols] = key_sum.astype(BF)
            dv_o[rows, cols] = value_sum.astype(BF)
        return carry

    lax.fori_loop(0, heads, collect, 0)

    for c in range(blocks):
        rows = slice(c * BLK, (c + 1) * BLK)
        ga_acc[rows, :] = part_send[z, rows, :].astype(F32)

        @pl.when(z > 0)
        def _():
            part_copy(z, c, True).wait_recv()
            ga_acc[rows, :] += from_below[z, rows, :].astype(F32)

        @pl.when(z < n_head - 1)
        def _():
            part_copy(z, c, False).wait_recv()
            ga_acc[rows, :] += from_above[z, rows, :].astype(F32)

        att_o[rows, :] = ga_acc[rows, :].astype(BF)

    def og_drain(c, carry):
        for step in range(n_head - 1):
            @pl.when((z - step >= 0) & (z < n_head - 1))
            def _():
                og_copy(z - step, c, True, False).wait_send()

            @pl.when((z + step < n_head) & (z > 0))
            def _():
                og_copy(z + step, c, False, False).wait_send()

        for d in range(n_head):
            @pl.when(z != d)
            def _():
                part_copy(d, c, True).wait_send()

        return carry

    lax.fori_loop(0, blocks, og_drain, 0)

    def seq_drain(i, carry):
        d = lax.rem(s_me + i, n_seq)
        k_copy(d).wait_send()
        v_copy(d).wait_send()

        def one(h, inner):
            ret_copy(h, d).wait_send()
            return inner

        return lax.fori_loop(0, heads, one, carry)

    lax.fori_loop(1, n_seq, seq_drain, 0)


def write_out(a0, a1, a2, a3, o0, o1, o2, o3, sems):
    copies = []
    for i, (src, dst) in enumerate(((a0, o0), (a1, o1), (a2, o2), (a3, o3))):
        for c in range(src.shape[0] // BLK):
            rows = pl.ds(c * BLK, BLK)
            copies.append(pltpu.make_async_copy(src.at[rows, :], dst.at[rows, :], sems.at[i, c]))
    for copy in copies:
        copy.start()
    for copy in copies:
        copy.wait()


def local(queries, key_states, value_states, block_lists, out_weight, out_grad):
    n_seq = lax.axis_size("seq")
    n_head = lax.axis_size("head")
    cells, width = queries.shape
    blocks = cells // BLK
    heads = width // HD
    slots = n_seq + blocks
    vmem = pl.BlockSpec(memory_space=pltpu.VMEM)
    main = pl.BlockSpec(memory_space=pltpu.HBM)
    sem = pltpu.SemaphoreType.DMA
    out = jax.ShapeDtypeStruct((cells, width), BF)
    held = pltpu.VMEM((cells, width), BF)
    results = pl.pallas_call(
        functools.partial(kernel, n_seq, n_head),
        out_shape=(held, held, held, held),
        in_specs=[
            main, main, main, main, main, main,
        ],
        out_specs=(vmem, vmem, vmem, vmem),
        scratch_shapes=[
            pltpu.VMEM((cells, width), BF),
            pltpu.VMEM((blocks, BLK, width), BF),
            pltpu.VMEM((blocks, BLK, width), BF),
            pltpu.VMEM((slots, BLK, width), BF),
            pltpu.VMEM((slots, BLK, width), BF),
            pltpu.VMEM((n_seq, BLK, width), BF),
            pltpu.VMEM((n_seq, BLK, width), BF),
            pltpu.VMEM(out_weight.shape, BF),
            pltpu.VMEM((n_head, cells, width), BF),
            pltpu.VMEM((heads, blocks, K_SEL + 1, BLK, BLK), BF),
            pltpu.VMEM((blocks, K_SEL + 1, BLK, BLK), BF),
            pltpu.VMEM((cells, width), BF),
            pltpu.VMEM((n_head, cells, width), BF),
            pltpu.VMEM((n_head, cells, width), BF),
            pltpu.VMEM((n_head, cells, width), BF),
            pltpu.VMEM((cells, width), F32),
            pltpu.VMEM((cells, width), BF),
            pltpu.VMEM((heads, n_seq, BLK, 2 * HD), BF),
            pltpu.VMEM((heads, n_seq, BLK, 2 * HD), BF),
            pltpu.VMEM((cells, width), F32),
            pltpu.VMEM((cells, width), F32),
            pltpu.SMEM(block_lists.shape[::-1], jnp.int32),
            pltpu.SMEM((blocks * K_SEL,), jnp.int32),
            pltpu.SMEM((n_seq,), jnp.int32),
            pltpu.SMEM((slots * blocks,), jnp.int32),
            sem((6,)), sem((n_head, blocks)), sem((n_head, blocks)), sem((n_head, blocks)),
            sem((n_seq,)), sem((n_seq,)), sem((n_seq,)), sem((n_seq,)),
            sem((n_head, blocks)), sem((n_head, blocks)), sem((n_head, blocks)),
            sem((heads, n_seq)), sem((heads, n_seq)),
        ],
        compiler_params=pltpu.CompilerParams(
            collective_id=0, has_side_effects=True, vmem_limit_bytes=56 * 1024 * 1024
        ),
        cost_estimate=pl.CostEstimate(
            flops=8 * 10**9, bytes_accessed=20 * 10**6, transcendentals=10**6
        ),
    )(
        block_lists.T,
        queries,
        key_states.reshape(blocks, BLK, width),
        value_states.reshape(blocks, BLK, width),
        out_grad,
        out_weight,
    )
    return pl.pallas_call(
        write_out,
        out_shape=(out, out, out, out),
        in_specs=[vmem] * 4,
        out_specs=(main,) * 4,
        scratch_shapes=[sem((4, blocks))],
        compiler_params=pltpu.CompilerParams(vmem_limit_bytes=8 * 1024 * 1024),
    )(*results)


def solution(mesh):
    in_specs = (
        P("seq", "head"),
        P("seq", "head"),
        P("seq", "head"),
        P(),
        P("head", None),
        P("seq", "head"),
    )
    out_specs = (P("seq", "head"), P("seq", "head"), P("seq", "head"), P("seq", "head"))
    return jax.shard_map(local, mesh=mesh, in_specs=in_specs, out_specs=out_specs, check_vma=False)
```
